256 devices in a mesh: ctx: 64 (over z, x, core), tp: 4 (over y).
Axes of the slice: x: 4, y: 4, z: 8, core: 2. Of those that a mesh axis runs over, the one named last changes fastest.
Arguments:
- inputs: bfloat16 [32768, 64, 128], P('ctx', 'tp'), may hold values from -6 to 6
- b_proj: bfloat16 [32768, 128], P('ctx'), may hold values from -0.5 to 0.5
- c_proj: bfloat16 [32768, 128], P('ctx'), may hold values from -0.5 to 0.5
- logdecay: float32 [32768, 64], P('ctx', 'tp'), may hold values from -1 to 0, as said below
- skip_gain: float32 [64], P('tp'), may hold values from 0.5 to 1.5
- grad_out: bfloat16 [32768, 64, 128], P('ctx', 'tp'), may hold values from -6 to 6
Outputs:
- outputs: bfloat16 [32768, 64, 128], P('ctx', 'tp')
- grad_inputs: bfloat16 [32768, 64, 128], P('ctx', 'tp')
- grad_logdecay: float32 [32768, 64], P('ctx', 'tp')
- grad_b: float32 [32768, 128], P('ctx')
- grad_c: float32 [32768, 128], P('ctx')
The draws below stay inside these ranges and needn't reach their ends.
Inputs may be any that keep to these rules, and one draw needn't show every extreme that they name: `logdecay`: non-positive log decays.
All inputs are finite; a program needn't handle non-finite values.
Results may differ from the reference program's by a relative error of at most 0.0025.
Values sent between devices are 32-bit elements; how exact they have to be, the bound alone decides.
No kernel may reach another device: no remote copies, remote signals or barrier semaphores. Data moves between devices by JAX's collectives and lax.ppermute only.
A program may use at most 320 MiB of HBM per device.

```python
import math
import jax
import jax.numpy as jnp
from jax import lax

HEAD_GROUP_COUNT = 64
HEAD_DIM = 128
STATE = 128
SPAN = 256
SEQUENCE_TOKENS = 32768


def draw_logdecay(key, part):
    key = jax.random.fold_in(key, 7)
    random_subkeys = jax.random.split(key, 6)
    fast_share = 0.5
    fast_heads = jax.random.uniform(random_subkeys[0], (HEAD_GROUP_COUNT,), jnp.float32) < fast_share
    fast_rate = jnp.exp(jax.random.uniform(random_subkeys[1], (HEAD_GROUP_COUNT,), jnp.float32, math.log(0.015), math.log(0.04)))
    slow_rate = jnp.exp(jax.random.uniform(random_subkeys[2], (HEAD_GROUP_COUNT,), jnp.float32, math.log(0.25 / SEQUENCE_TOKENS), math.log(2.0 / SEQUENCE_TOKENS)))
    decay_rate = jnp.where(fast_heads, fast_rate, slow_rate)
    step_sizes = jnp.exp(jax.random.uniform(random_subkeys[3], (SEQUENCE_TOKENS, HEAD_GROUP_COUNT), jnp.float32, math.log(0.5), math.log(2.0)))
    surge_locations = jax.random.randint(random_subkeys[4], (4,), 0, SEQUENCE_TOKENS)
    random_surge = jnp.any(jnp.arange(SEQUENCE_TOKENS)[:, None] == surge_locations[None, :], axis=1)
    surge_extent = jax.random.uniform(random_subkeys[5], (SEQUENCE_TOKENS, HEAD_GROUP_COUNT), jnp.float32, math.log(0.5), math.log(0.8))
    starting_value = -decay_rate[None, :] * step_sizes
    return jnp.where(random_surge[:, None], starting_value + surge_extent, starting_value).astype(jnp.float32)


def shard_levels(stream_key, dims, cuts, low, high):
    def one(position, blocks):
        heights = jax.random.uniform(jax.random.fold_in(jax.random.fold_in(stream_key, 6), position), (blocks,), jnp.float32, low / len(cuts), high / len(cuts))
        return jnp.repeat(jnp.exp(heights), dims[position] // blocks).reshape((-1,) + (1,) * (len(dims) - position - 1))

    loudness = one(*cuts[0])
    for cut in cuts[1:]:
        loudness = loudness * one(*cut)
    return loudness


def gaussian(own_key, shape, deviation, limit, shards=(), held_as=jnp.bfloat16):
    result = jax.random.normal(own_key, shape, jnp.float32) * deviation
    if len(shards) > 0:
        result = shard_levels(own_key, shape, shards, -0.22, 0.18) * result
    return jnp.clip(result, min=-limit, max=limit).astype(held_as)


def setup_inputs(seed: int = 0) -> dict:
    key_list = jax.random.split(jax.random.key(seed), 7)
    return {
        "inputs": gaussian(key_list[0], (SEQUENCE_TOKENS, HEAD_GROUP_COUNT, HEAD_DIM), 1.0, 6.0, ((0, 64), (1, 4))),
        "b_proj": gaussian(key_list[1], (SEQUENCE_TOKENS, STATE), STATE ** -0.5, 0.5, ((0, 64),)),
        "c_proj": gaussian(key_list[2], (SEQUENCE_TOKENS, STATE), STATE ** -0.5, 0.5, ((0, 64),)),
        "logdecay": draw_logdecay(jax.random.fold_in(key_list[6], 71), 0),
        "skip_gain": jnp.clip(1.0 + 0.1 * jax.random.normal(key_list[4], (HEAD_GROUP_COUNT,), jnp.float32), 0.5, 1.5),
        "grad_out": gaussian(key_list[5], (SEQUENCE_TOKENS, HEAD_GROUP_COUNT, HEAD_DIM), 1.0, 6.0, ((0, 64), (1, 4))),
    }


highest = lax.Precision.HIGHEST


def span_terms(b_rows, c_rows, x_rows, dy_rows, log_rows):
    levels = jnp.cumsum(log_rows, axis=0)
    finals = levels[-1]
    causal = jnp.arange(SPAN)[:, None] >= jnp.arange(SPAN)[None, :]
    scores = jnp.dot(c_rows, b_rows.T, preferred_element_type=jnp.float32)
    levels_t = levels.T
    distance = levels_t[:, :, None] - levels_t[:, None, :]
    decay_mat = jnp.where(causal[None], jnp.exp(jnp.where(causal[None], distance, 0.0)), 0.0)
    mixing = (scores[None] * decay_mat).astype(jnp.bfloat16)
    mix32 = mixing.astype(jnp.float32)
    x32 = x_rows.astype(jnp.float32)
    dy32 = dy_rows.astype(jnp.float32)
    b32 = b_rows.astype(jnp.float32)
    c32 = c_rows.astype(jnp.float32)
    y_intra = jnp.einsum("hts,shp->thp", mix32, x32, precision=highest)
    dx_intra = jnp.einsum("hts,thp->shp", mix32, dy32, precision=highest)
    to_end = jnp.exp(finals[None, :] - levels)
    head_w = jnp.exp(levels)
    weighted_x = x32 * to_end[:, :, None]
    weighted_dy = dy32 * head_w[:, :, None]
    pair_dot = jnp.einsum("thp,shp->hts", dy32, x32, precision=highest)
    score_grad = jnp.sum(pair_dot * decay_mat, axis=0)
    gb_intra = jnp.dot(score_grad.T, c32, precision=highest)
    gc_intra = jnp.dot(score_grad, b32, precision=highest)
    return finals, b32, c32, x32, dy32, y_intra, dx_intra, weighted_x, weighted_dy, head_w, to_end, gb_intra, gc_intra


def reference(inputs, b_proj, c_proj, logdecay, skip_gain, grad_out):
    nchunk = SEQUENCE_TOKENS // SPAN
    xs = inputs.reshape(nchunk, SPAN, HEAD_GROUP_COUNT, HEAD_DIM)
    dys = grad_out.reshape(nchunk, SPAN, HEAD_GROUP_COUNT, HEAD_DIM)
    bs = b_proj.reshape(nchunk, SPAN, STATE)
    cs = c_proj.reshape(nchunk, SPAN, STATE)
    logs = logdecay.reshape(nchunk, SPAN, HEAD_GROUP_COUNT)

    def forward_step(state_now, pieces):
        b_rows, c_rows, x_rows, dy_rows, log_rows = pieces
        finals, b32, c32, x32, dy32, y_intra, dx_intra, weighted_x, weighted_dy, head_w, to_end, gb_intra, gc_intra = span_terms(b_rows, c_rows, x_rows, dy_rows, log_rows)
        y_inter = jnp.einsum("tn,hnp->thp", c32, state_now, precision=highest) * head_w[:, :, None]
        y_local = y_intra + y_inter
        y_out = (y_local + skip_gain[None, :, None] * x32).astype(jnp.bfloat16)
        y_dot = jnp.sum(y_local * dy32, axis=2)
        gc_inter = jnp.einsum("hnp,thp->tn", state_now, weighted_dy, precision=highest)
        fresh_state = jnp.einsum("sn,shp->hnp", b32, weighted_x, precision=highest)
        state_next = jnp.exp(finals)[:, None, None] * state_now + fresh_state
        return state_next, (y_out, y_dot, gc_intra + gc_inter)

    def backward_step(grad_next, pieces):
        b_rows, c_rows, x_rows, dy_rows, log_rows = pieces
        finals, b32, c32, x32, dy32, y_intra, dx_intra, weighted_x, weighted_dy, head_w, to_end, gb_intra, gc_intra = span_terms(b_rows, c_rows, x_rows, dy_rows, log_rows)
        dx_inter = jnp.einsum("sn,hnp->shp", b32, grad_next, precision=highest) * to_end[:, :, None]
        dx_local = dx_intra + dx_inter
        dx_out = (dx_local + skip_gain[None, :, None] * dy32).astype(jnp.bfloat16)
        x_dot = jnp.sum(dx_local * x32, axis=2)
        gb_inter = jnp.einsum("hnp,shp->sn", grad_next, weighted_x, precision=highest)
        pulled = jnp.einsum("tn,thp->hnp", c32, weighted_dy, precision=highest)
        grad_now = pulled + jnp.exp(finals)[:, None, None] * grad_next
        return grad_now, (dx_out, x_dot, gb_intra + gb_inter)

    zeros_state = jnp.zeros((HEAD_GROUP_COUNT, STATE, HEAD_DIM), jnp.float32)
    pieces = (bs, cs, xs, dys, logs)
    unused_a, (y_all, y_dots, grad_c) = lax.scan(forward_step, zeros_state, pieces)
    unused_b, (dx_all, x_dots, grad_b) = lax.scan(backward_step, zeros_state, pieces, reverse=True)
    crossing = (y_dots - x_dots).reshape(SEQUENCE_TOKENS, HEAD_GROUP_COUNT)
    grad_logdecay = -(jnp.cumsum(crossing, axis=0) - crossing)
    outputs = y_all.reshape(SEQUENCE_TOKENS, HEAD_GROUP_COUNT, HEAD_DIM)
    grad_inputs = dx_all.reshape(SEQUENCE_TOKENS, HEAD_GROUP_COUNT, HEAD_DIM)
    return outputs, grad_inputs, grad_logdecay, grad_b.reshape(SEQUENCE_TOKENS, STATE), grad_c.reshape(SEQUENCE_TOKENS, STATE)
```

```python
import functools

import jax
import jax.numpy as jnp
from jax import lax
from jax.experimental import pallas as pl
from jax.experimental.pallas import tpu as pltpu
from jax.sharding import PartitionSpec as P

SPAN = 256
HEADS = 16
HALF = 8
WIDTH = 128
CHIPS = 4
QUAD = 4
LOG_ROWS = 8
f32 = jnp.float32
bf16 = jnp.bfloat16
vmem = pl.BlockSpec(memory_space=pltpu.VMEM)


def params():
    return pltpu.CompilerParams(vmem_limit_bytes=48 * 1024 * 1024)


def place():
    position = lax.axis_index("ctx")
    return position % 2, position // 2 % 4, position // 8


def dot(a, b, dims):
    return lax.dot_general(a, b, (dims, ((), ())), preferred_element_type=f32)


def split_two(a):
    high = a.astype(bf16)
    return high, (a - high.astype(f32)).astype(bf16)


def split_three(a):
    high = a.astype(bf16)
    rest = a - high.astype(f32)
    middle = rest.astype(bf16)
    return high, middle, (rest - middle.astype(f32)).astype(bf16)


def triangle(strict):
    row = lax.broadcasted_iota(jnp.int32, (SPAN, SPAN), 0)
    column = lax.broadcasted_iota(jnp.int32, (SPAN, SPAN), 1)
    kept = column < row if strict else column <= row
    return jnp.where(kept, 1.0, 0.0).astype(bf16)


def running_sum(a, strict):
    tri = triangle(strict)
    return sum(dot(tri, part, ((1,), (0,))) for part in split_three(a))


def slot_of(head):
    core, chip, _ = place()
    half = head // HALF
    group = head % HALF // 2
    return jnp.where(half == core, HALF, 0) + (group - chip + 4) % 4 * 2 + head % 2


def summary_body(reverse, values, proj, logdecay, heads_out, send, keep, middle, *rest):
    if reverse:
        wide, total = rest
    else:
        levels_out, levels_rows_out, wide, total = rest
    step = pl.program_id(0)
    span = 1 - step if reverse else step
    log_span = logdecay[pl.ds(pl.multiple_of(span * SPAN, SPAN), SPAN), :]
    levels = running_sum(log_span, False)
    if not reverse:
        levels_out[...] = levels
        levels_rows_out[...] = jnp.transpose(levels)
    last = levels[SPAN - 1 : SPAN, :]
    weight = jnp.exp(levels) if reverse else jnp.exp(last - levels)
    carried = jnp.where(step == 0, 0.0, jnp.exp(last))
    all_log = jnp.sum(logdecay[...], axis=0, keepdims=True)
    proj_t = jnp.transpose(proj[...])
    wide[...] = values[...].reshape(SPAN * HEADS, WIDTH).astype(f32)

    @pl.when(step == 0)
    def _():
        total[...] = jnp.zeros_like(total)

    for head in range(HEADS):
        rows = wide[pl.ds(head, SPAN, stride=HEADS), :]
        heads_out[head] = rows.astype(bf16)
        high, low = split_two(rows * weight[:, head : head + 1])
        both = dot(proj_t, jnp.concatenate([high, low], axis=1), ((1,), (0,)))
        slot = slot_of(head)
        fresh = both[:, :WIDTH] + both[:, WIDTH:]
        total[slot, :WIDTH, :] = fresh + carried[:, head : head + 1] * total[slot, :WIDTH, :]
        total[slot, WIDTH:, :] = jnp.broadcast_to(all_log[:, head : head + 1], (LOG_ROWS, WIDTH))

        @pl.when(step == 0)
        def _():
            middle[head] = fresh

    @pl.when(step == 1)
    def _():
        send[...] = total[:HALF]
        keep[...] = total[HALF:]


def summary(reverse, values, proj, logdecay):
    tokens = values.shape[0]

    def turn(step):
        return 1 - step if reverse else step

    packed = jax.ShapeDtypeStruct((HALF, WIDTH + LOG_ROWS, WIDTH), f32)
    packed_spec = pl.BlockSpec((HALF, WIDTH + LOG_ROWS, WIDTH), lambda s: (0, 0, 0))
    shapes = [
        jax.ShapeDtypeStruct((HEADS, tokens, WIDTH), bf16),
        packed,
        packed,
        jax.ShapeDtypeStruct((HEADS, WIDTH, WIDTH), f32),
    ]
    specs = [
        pl.BlockSpec((HEADS, SPAN, WIDTH), lambda s: (0, turn(s), 0)),
        packed_spec,
        packed_spec,
        pl.BlockSpec((HEADS, WIDTH, WIDTH), lambda s: (0, 0, 0)),
    ]
    if not reverse:
        shapes += [
            jax.ShapeDtypeStruct((tokens, HEADS), f32),
            jax.ShapeDtypeStruct((HEADS, tokens), f32),
        ]
        specs += [
            pl.BlockSpec((SPAN, HEADS), lambda s: (turn(s), 0)),
            pl.BlockSpec((HEADS, SPAN), lambda s: (0, turn(s))),
        ]
    return pl.pallas_call(
        functools.partial(summary_body, reverse),
        grid=(2,),
        in_specs=[
            pl.BlockSpec((SPAN, HEADS, WIDTH), lambda s: (turn(s), 0, 0)),
            pl.BlockSpec((SPAN, WIDTH), lambda s: (turn(s), 0)),
            pl.BlockSpec((tokens, HEADS), lambda s: (0, 0)),
        ],
        out_specs=specs,
        out_shape=shapes,
        scratch_shapes=[
            pltpu.VMEM((SPAN * HEADS, WIDTH), f32),
            pltpu.VMEM((HEADS, WIDTH + LOG_ROWS, WIDTH), f32),
        ],
        compiler_params=params(),
        name="summary_b" if reverse else "summary_f",
    )(values, proj, logdecay)


def intra_body(x_ref, dy_ref, b_ref, c_ref, lev_ref, lev_rows_ref, gain_ref, y_out, dx_out, cross_out, gb_out, gc_out):
    b = b_ref[...]
    c = c_ref[...]
    low, high = slice(0, 128), slice(128, 256)
    blocks = ((low, low), (high, low), (high, high))
    scores = [dot(c[t], b[s], ((1,), (1,))) for t, s in blocks]
    row = lax.broadcasted_iota(jnp.int32, (128, 128), 0)
    column = lax.broadcasted_iota(jnp.int32, (128, 128), 1)
    causal = column <= row
    lane = lax.broadcasted_iota(jnp.int32, (SPAN, HEADS), 1)
    score_grad = [jnp.zeros((128, 128), f32) for _ in blocks]
    cross = jnp.zeros((SPAN, HEADS), f32)
    for head in range(HEADS):
        x = x_ref[head]
        dy = dy_ref[head]
        gain = gain_ref[:, head : head + 1]
        level = lev_ref[:, head : head + 1]
        level_row = lev_rows_ref[head : head + 1, :]
        mixing = []
        for at, (t, s) in enumerate(blocks):
            distance = level[t] - level_row[:, s]
            if t == s:
                distance = jnp.where(causal, distance, -1e30)
            decay = jnp.exp(distance)
            mixing.append((scores[at] * decay).astype(bf16))
            score_grad[at] = score_grad[at] + decay * dot(dy[t], x[s], ((1,), (1,)))
        lower = jnp.concatenate(mixing[1:], axis=1)
        left = jnp.concatenate(mixing[:2], axis=0)
        y = jnp.concatenate([dot(mixing[0], x[low], ((1,), (0,))), dot(lower, x, ((1,), (0,)))], axis=0)
        dx = jnp.concatenate([dot(left, dy, ((0,), (0,))), dot(mixing[2], dy[high], ((0,), (0,)))], axis=0)
        x32 = x.astype(f32)
        dy32 = dy.astype(f32)
        line = jnp.sum(y * dy32 - dx * x32, axis=1, keepdims=True)
        cross = jnp.where(lane == head, line, cross)
        y_out[head] = y + gain * x32
        dx_out[head] = dx + gain * dy32
    cross_out[...] = cross
    g00, g10, g11 = [split_two(g) for g in score_grad]
    gc_out[low, :] = sum(dot(g, b[low], ((1,), (0,))) for g in g00)
    gc_out[high, :] = sum(dot(g, b[low], ((1,), (0,))) for g in g10) + sum(dot(g, b[high], ((1,), (0,))) for g in g11)
    gb_out[low, :] = sum(dot(g, c[low], ((0,), (0,))) for g in g00) + sum(dot(g, c[high], ((0,), (0,))) for g in g10)
    gb_out[high, :] = sum(dot(g, c[high], ((0,), (0,))) for g in g11)


def intra(x_heads, dy_heads, b_proj, c_proj, levels, level_rows, gain):
    tokens = x_heads.shape[1]
    by_head = pl.BlockSpec((HEADS, SPAN, WIDTH), lambda s: (0, s, 0))
    flat = pl.BlockSpec((SPAN, WIDTH), lambda s: (s, 0))
    thin = pl.BlockSpec((SPAN, HEADS), lambda s: (s, 0))
    return pl.pallas_call(
        intra_body,
        grid=(2,),
        in_specs=[
            by_head,
            by_head,
            flat,
            flat,
            thin,
            pl.BlockSpec((HEADS, SPAN), lambda s: (0, s)),
            pl.BlockSpec((1, HEADS), lambda s: (0, 0)),
        ],
        out_specs=[by_head, by_head, thin, flat, flat],
        out_shape=[
            jax.ShapeDtypeStruct((HEADS, tokens, WIDTH), f32),
            jax.ShapeDtypeStruct((HEADS, tokens, WIDTH), f32),
            jax.ShapeDtypeStruct((tokens, HEADS), f32),
            jax.ShapeDtypeStruct((tokens, WIDTH), f32),
            jax.ShapeDtypeStruct((tokens, WIDTH), f32),
        ],
        compiler_params=params(),
        name="intra",
    )(x_heads, dy_heads, b_proj, c_proj, levels, level_rows, gain)


def weigh(orders, logs, after, before):
    exponent = jnp.zeros_like(logs[0])
    for order, log in zip(orders, logs):
        exponent = exponent + jnp.where((order > after) & (order < before), log, 0.0)
    return jnp.exp(exponent)


def ranks(reverse, mine):
    spots = [(mine - k + 4) % 4 for k in range(4)]
    return [3 - spot for spot in spots] if reverse else spots


def whole_of(orders, logs, states):
    return sum(weigh(orders, logs, order, 4) * state for order, state in zip(orders, states))


def prefix_of(orders, logs, states, at, entering):
    out = weigh(orders, logs, -1, orders[at]) * entering
    for k in range(4):
        if k != at:
            weight = weigh(orders, logs, orders[k], orders[at])
            out = out + jnp.where(orders[k] < orders[at], weight, 0.0) * states[k]
    return out


def small(body, outs, name, scratch=()):
    return pl.pallas_call(
        body,
        out_shape=[jax.ShapeDtypeStruct(shape, f32) for shape in outs],
        scratch_shapes=[pltpu.VMEM(shape, f32) for shape in scratch],
        compiler_params=params(),
        name=name,
    )


def core_first(reverse):
    core, _, _ = place()
    return core == (1 if reverse else 0)


def core_up_body(reverse, keep, other, *outs):
    first = core_first(reverse)
    for head in range(HALF):
        own_log = keep[head, WIDTH : WIDTH + 1, :]
        other_log = other[head, WIDTH : WIDTH + 1, :]
        own_weight = jnp.exp(jnp.where(first, other_log, 0.0))
        other_weight = jnp.exp(jnp.where(first, 0.0, own_log))
        out = outs[head // 2]
        out[head % 2, :WIDTH, :] = own_weight * keep[head, :WIDTH, :] + other_weight * other[head, :WIDTH, :]
        out[head % 2, WIDTH:, :] = keep[head, WIDTH:, :] + other[head, WIDTH:, :]


def chip_up_body(reverse, *refs):
    parts, outs, units = refs[:4], refs[4:8], refs[8]
    _, chip, depth = place()
    orders = ranks(reverse, chip)
    for head in range(2):
        logs = [part[head, WIDTH : WIDTH + 1, :] for part in parts]
        state = whole_of(orders, logs, [part[head, :WIDTH, :] for part in parts])
        log = jnp.broadcast_to(sum(logs), (LOG_ROWS, WIDTH))
        for side in range(2):
            units[2 * head + side, :64, :] = state[64 * side : 64 * side + 64]
            units[2 * head + side, 64:, :] = log
    for k in range(4):
        outs[k][...] = units[(depth + k) % 4]


def depth_up_body(reverse, *refs):
    parts, out = refs[:4], refs[4]
    orders = ranks(reverse, place()[2] % 4)
    logs = [part[64:65, :] for part in parts]
    out[...] = whole_of(orders, logs, [part[:64, :] for part in parts])


def depth_down_body(reverse, *refs):
    parts, entering, outs = refs[:4], refs[4], refs[5:]
    orders = ranks(reverse, place()[2] % 4)
    logs = [part[64:65, :] for part in parts]
    states = [part[:64, :] for part in parts]
    for k in range(4):
        outs[k][...] = prefix_of(orders, logs, states, k, entering[...])


def chip_down_body(reverse, *refs):
    parts, pieces, outs, units = refs[:4], refs[4:8], refs[8:12], refs[12]
    _, chip, depth = place()
    orders = ranks(reverse, chip)
    for k in range(4):
        units[(depth + k) % 4] = pieces[k][...]
    for head in range(2):
        entering = units[2 * head : 2 * head + 2].reshape(WIDTH, WIDTH)
        logs = [part[head, WIDTH : WIDTH + 1, :] for part in parts]
        states = [part[head, :WIDTH, :] for part in parts]
        for k in range(4):
            outs[k][head] = prefix_of(orders, logs, states, k, entering)


def core_down_body(reverse, keep, other, *refs):
    pieces, mine, theirs = refs[:4], refs[4], refs[5]
    first = core_first(reverse)
    for head in range(HALF):
        entering = pieces[head // 2][head % 2]
        own_log = keep[head, WIDTH : WIDTH + 1, :]
        other_log = other[head, WIDTH : WIDTH + 1, :]
        mine[head] = jnp.where(first, entering, jnp.exp(other_log) * entering + other[head, :WIDTH, :])
        theirs[head] = jnp.where(first, jnp.exp(own_log) * entering + keep[head, :WIDTH, :], entering)


def over_ctx(array, target):
    pairs = [(i, target(i)) for i in range(64)]
    return lax.ppermute(array, "ctx", [pair for pair in pairs if pair[1] is not None])


def swap_cores(array):
    return over_ctx(array, lambda i: i ^ 1)


def along_x(array, k):
    return over_ctx(array, lambda i: i // 8 * 8 + (i // 2 + k) % 4 * 2 + i % 2)


def along_z(array, k):
    return over_ctx(array, lambda i: i // 32 * 32 + (i // 8 + k) % 4 * 8 + i % 8)


def across_z(reverse, array):
    if reverse:
        return over_ctx(array, lambda i: i - 32 if i >= 32 else None)
    return over_ctx(array, lambda i: i + 32 if i < 32 else None)


def scan(reverse, send, keep):
    tag = "_b" if reverse else "_f"
    packed = (2, WIDTH + LOG_ROWS, WIDTH)
    plain = (2, WIDTH, WIDTH)
    unit = (64, WIDTH)
    packed_unit = (64 + LOG_ROWS, WIDTH)

    def call(body, outs, name, *args, scratch=()):
        return small(functools.partial(body, reverse), outs, name + tag, scratch)(*args)

    other = swap_cores(send)
    parts = call(core_up_body, [packed] * 4, "core_up", keep, other)
    parts = [parts[0]] + [along_x(parts[k], k) for k in (1, 2, 3)]
    units = call(chip_up_body, [packed_unit] * 4, "chip_up", *parts, scratch=[(4,) + packed_unit])
    units = [units[0]] + [along_z(units[k], k) for k in (1, 2, 3)]
    (quad,) = call(depth_up_body, [unit], "depth_up", *units)
    quad = across_z(reverse, quad)
    back = call(depth_down_body, [unit] * 4, "depth_down", *units, quad)
    back = [back[0]] + [along_z(back[k], -k) for k in (1, 2, 3)]
    entering = call(chip_down_body, [plain] * 4, "chip_down", *parts, *back, scratch=[(4,) + unit])
    entering = [entering[0]] + [along_x(entering[k], -k) for k in (1, 2, 3)]
    mine, theirs = call(core_down_body, [(HALF, WIDTH, WIDTH)] * 2, "core_down", keep, other, *entering)
    return swap_cores(theirs), mine


def state_at(span, reverse, head, got, mine, middle, levels_all):
    slot = slot_of(head)
    near = jnp.where(slot >= HALF, mine[slot % HALF], got[slot % HALF])
    row = 2 * SPAN - 1 if reverse else SPAN - 1
    second = span == (0 if reverse else 1)
    crossed = jnp.exp(levels_all[row : row + 1, head : head + 1])
    return jnp.where(second, crossed * near + middle[head], near)


def row_weight(reverse, levels):
    return jnp.exp(levels[SPAN - 1 : SPAN, :] - levels) if reverse else jnp.exp(levels)


def grad_body(reverse, got, mine, middle, levels_all, levels_ref, values, base, *refs):
    outs, total = refs[:4], refs[4]
    span = pl.program_id(0)
    weight = row_weight(reverse, levels_ref[...])
    acc = base[...]
    for head in range(HEADS):
        state = state_at(span, reverse, head, got, mine, middle, levels_all)
        value = values[head]
        line = dot(
            jnp.concatenate([value, value], axis=1),
            jnp.concatenate(split_two(state), axis=1),
            ((1,), (1,)),
        )
        acc = acc + weight[:, head : head + 1] * line
    total[pl.ds(pl.multiple_of(span * SPAN, SPAN), SPAN), :] = acc

    @pl.when(span == 1)
    def _():
        mine_tp = lax.axis_index("tp")
        for k in range(4):
            start = pl.multiple_of((mine_tp + k) % 4 * 128, 128)
            outs[k][...] = total[pl.ds(start, 128), :]


def grad_call(reverse, got, mine, middle, levels, values, base):
    tokens = levels.shape[0]
    states = pl.BlockSpec((HALF, WIDTH, WIDTH), lambda s: (0, 0, 0))
    piece = pl.BlockSpec((tokens // 4, WIDTH), lambda s: (0, 0))
    return pl.pallas_call(
        functools.partial(grad_body, reverse),
        grid=(2,),
        in_specs=[
            states,
            states,
            pl.BlockSpec((HEADS, WIDTH, WIDTH), lambda s: (0, 0, 0)),
            pl.BlockSpec((tokens, HEADS), lambda s: (0, 0)),
            pl.BlockSpec((SPAN, HEADS), lambda s: (s, 0)),
            pl.BlockSpec((HEADS, SPAN, WIDTH), lambda s: (0, s, 0)),
            pl.BlockSpec((SPAN, WIDTH), lambda s: (s, 0)),
        ],
        out_specs=[piece] * 4,
        out_shape=[jax.ShapeDtypeStruct((tokens // 4, WIDTH), f32)] * 4,
        scratch_shapes=[pltpu.VMEM((tokens, WIDTH), f32)],
        compiler_params=params(),
        name="grad_b" if reverse else "grad_c",
    )(got, mine, middle, levels, levels, values, base)


def value_body(reverse, got, mine, middle, levels_all, levels_ref, proj, partial_ref, values, out, cross_out, wide):
    span = pl.program_id(0)
    weight = row_weight(reverse, levels_ref[...])
    doubled = jnp.concatenate([proj[...], proj[...]], axis=1)
    lane = lax.broadcasted_iota(jnp.int32, (SPAN, HEADS), 1)
    cross = jnp.zeros((SPAN, HEADS), f32)
    for head in range(HEADS):
        state = state_at(span, reverse, head, got, mine, middle, levels_all)
        far = dot(doubled, jnp.concatenate(split_two(state), axis=0), ((1,), (0,)))
        far = far * weight[:, head : head + 1]
        line = jnp.sum(far * values[head].astype(f32), axis=1, keepdims=True)
        cross = jnp.where(lane == head, line, cross)
        wide[pl.ds(head, SPAN, stride=HEADS), :] = partial_ref[head] + far
    out[...] = wide[...].astype(bf16).reshape(SPAN, HEADS, WIDTH)
    cross_out[...] = cross


def value_call(reverse, got, mine, middle, levels, proj, partial_sum, values):
    tokens = levels.shape[0]
    states = pl.BlockSpec((HALF, WIDTH, WIDTH), lambda s: (0, 0, 0))
    by_head = pl.BlockSpec((HEADS, SPAN, WIDTH), lambda s: (0, s, 0))
    thin = pl.BlockSpec((SPAN, HEADS), lambda s: (s, 0))
    return pl.pallas_call(
        functools.partial(value_body, reverse),
        grid=(2,),
        in_specs=[
            states,
            states,
            pl.BlockSpec((HEADS, WIDTH, WIDTH), lambda s: (0, 0, 0)),
            pl.BlockSpec((tokens, HEADS), lambda s: (0, 0)),
            thin,
            pl.BlockSpec((SPAN, WIDTH), lambda s: (s, 0)),
            by_head,
            by_head,
        ],
        out_specs=[pl.BlockSpec((SPAN, HEADS, WIDTH), lambda s: (s, 0, 0)), thin],
        out_shape=[
            jax.ShapeDtypeStruct((tokens, HEADS, WIDTH), bf16),
            jax.ShapeDtypeStruct((tokens, HEADS), f32),
        ],
        scratch_shapes=[pltpu.VMEM((SPAN * HEADS, WIDTH), f32)],
        compiler_params=params(),
        name="values_b" if reverse else "values_f",
    )(got, mine, middle, levels, levels, proj, partial_sum, values)


def decay_body(near, forward, backward, levels, got_f, mine_f, got_b, mine_b, send_b, keep_b, out):
    lane = lax.broadcasted_iota(jnp.int32, (1, HEADS), 1)
    start = jnp.zeros((1, HEADS), f32)
    for head in range(HEADS):
        slot = slot_of(head)
        at = slot % HALF
        own = slot >= HALF
        entering = jnp.where(own, mine_f[at], got_f[at])
        beyond = jnp.where(own, mine_b[at], got_b[at])
        local = jnp.where(own, keep_b[at], send_b[at])
        pulled = local[:WIDTH] + jnp.exp(local[WIDTH : WIDTH + 1]) * beyond
        line = jnp.sum(jnp.sum(entering * pulled, axis=0, keepdims=True), axis=1, keepdims=True)
        start = jnp.where(lane == head, line, start)
    for span in range(2):
        rows = slice(span * SPAN, span * SPAN + SPAN)
        cross = near[rows, :] + forward[rows, :] - backward[rows, :]
        out[rows, :] = start - running_sum(cross, True)
        start = start - jnp.sum(cross, axis=0, keepdims=True)


def decay_call(near, forward, backward, levels, *states):
    return small(decay_body, [near.shape], "decay")(near, forward, backward, levels, *states)[0]


def over_tp(array, k):
    return lax.ppermute(array, "tp", [(i, (i + k) % 4) for i in range(4)])


def join_body(p0, p1, p2, p3, out):
    mine = lax.axis_index("tp")
    for k, piece in enumerate((p0, p1, p2, p3)):
        out[pl.ds(pl.multiple_of((mine - k + 4) % 4 * 128, 128), 128), :] = piece[...]


def sum_tp(pieces, name):
    total = pieces[0]
    for k in (1, 2, 3):
        total = total + over_tp(pieces[k], k)
    rows, width = total.shape
    joined = [total] + [over_tp(total, k) for k in (1, 2, 3)]
    return small(join_body, [(4 * rows, width)], name)(*joined)[0]


def on_device(inputs, b_proj, c_proj, logdecay, skip_gain, grad_out):
    x_heads, send_f, keep_f, middle_f, levels, level_rows = summary(False, inputs, b_proj, logdecay)
    dy_heads, send_b, keep_b, middle_b = summary(True, grad_out, c_proj, logdecay)
    got_f, mine_f = scan(False, send_f, keep_f)
    got_b, mine_b = scan(True, send_b, keep_b)
    y_part, dx_part, near, grad_b, grad_c = intra(
        x_heads, dy_heads, b_proj, c_proj, levels, level_rows, skip_gain.reshape(1, HEADS)
    )
    grad_c = sum_tp(grad_call(False, got_f, mine_f, middle_f, levels, dy_heads, grad_c), "join_c")
    outputs, cross_f = value_call(False, got_f, mine_f, middle_f, levels, c_proj, y_part, dy_heads)
    grad_b = sum_tp(grad_call(True, got_b, mine_b, middle_b, levels, x_heads, grad_b), "join_b")
    grad_inputs, cross_b = value_call(True, got_b, mine_b, middle_b, levels, b_proj, dx_part, x_heads)
    grad_logdecay = decay_call(near, cross_f, cross_b, levels, got_f, mine_f, got_b, mine_b, send_b, keep_b)
    return outputs, grad_inputs, grad_logdecay, grad_b, grad_c


def solution(mesh):
    placed = (
        P("ctx", "tp", None),
        P("ctx", None),
        P("ctx", None),
        P("ctx", "tp"),
        P("tp"),
        P("ctx", "tp", None),
    )
    return jax.shard_map(
        on_device,
        mesh=mesh,
        in_specs=placed,
        out_specs=(
            P("ctx", "tp", None),
            P("ctx", "tp", None),
            P("ctx", "tp"),
            P("ctx", None),
            P("ctx", None),
        ),
        check_vma=False,
    )
```

```python
import functools

import jax
import jax.numpy as jnp
from jax import lax
from jax.experimental import pallas as pl
from jax.experimental.pallas import tpu as pltpu
from jax.sharding import PartitionSpec as P

SPAN = 256
HEADS = 16
HALF = 8
WIDTH = 128
CHIPS = 4
QUAD = 4
LOG_ROWS = 8
f32 = jnp.float32
bf16 = jnp.bfloat16
TALL = 2 * WIDTH + LOG_ROWS
anywhere = pl.BlockSpec(memory_space=pl.ANY)


def params():
    return pltpu.CompilerParams(vmem_limit_bytes=24 * 1024 * 1024)


def place():
    position = lax.axis_index("ctx")
    return position % 2, position // 2 % 4, position // 8


def dot(a, b, dims):
    return lax.dot_general(a, b, (dims, ((), ())), preferred_element_type=f32)


def split_two(a):
    high = a.astype(bf16)
    return high, (a - high.astype(f32)).astype(bf16)


def split_three(a):
    high = a.astype(bf16)
    rest = a - high.astype(f32)
    middle = rest.astype(bf16)
    return high, middle, (rest - middle.astype(f32)).astype(bf16)


def triangle(strict):
    row = lax.broadcasted_iota(jnp.int32, (SPAN, SPAN), 0)
    column = lax.broadcasted_iota(jnp.int32, (SPAN, SPAN), 1)
    kept = column < row if strict else column <= row
    return jnp.where(kept, 1.0, 0.0).astype(bf16)


def running_sum(rows, strict):
    tri = triangle(strict)
    return sum(dot(part, tri, ((1,), (1,))) for part in split_three(rows))


def slot_of(head):
    _, chip, _ = place()
    return (head % HALF // 2 - chip + 4) % 4 * 2 + head % 2


def summary_body(reverse, values, proj, logdecay, *refs):
    if reverse:
        heads_out, send, keep, middle, stage = refs
    else:
        heads_out, send, keep, middle, levels_out, level_rows_out, stage = refs
    step = pl.program_id(0)
    span = 1 - step if reverse else step
    level_rows = running_sum(logdecay[:, pl.ds(pl.multiple_of(span * SPAN, SPAN), SPAN)], False)
    if not reverse:
        levels_out[...] = jnp.transpose(level_rows)
        level_rows_out[...] = level_rows
    weight = jnp.exp(level_rows) if reverse else jnp.exp(level_rows[:, SPAN - 1 : SPAN] - level_rows)
    proj_t = jnp.transpose(proj[...]).astype(f32)
    swapped = jnp.swapaxes(values[...], 0, 1)
    heads_out[...] = swapped
    for head in range(HEADS):
        weighted = jnp.concatenate(split_two(proj_t * weight[head : head + 1, :]), axis=0)
        both = dot(weighted, swapped[head], ((1,), (0,)))
        stage[step, head] = both[:WIDTH] + both[WIDTH:]

    @pl.when(step == 1)
    def _():
        core, _, _ = place()
        carried = jnp.exp(level_rows[:, SPAN - 1 : SPAN])
        all_log = jnp.sum(logdecay[...], axis=1, keepdims=True)
        middle[...] = stage[0]
        for own, out in ((False, send), (True, keep)):
            half = core if own else 1 - core
            crossed = jnp.where(half == 0, carried[:HALF], carried[HALF:])
            log = jnp.where(half == 0, all_log[:HALF], all_log[HALF:])
            for at in range(HALF):
                slot = slot_of(at)
                head = half * HALF + at
                out[slot, :WIDTH, :] = stage[1, head] + crossed[at : at + 1, :] * stage[0, head]
                if not reverse:
                    out[slot, WIDTH:, :] = jnp.broadcast_to(log[at : at + 1, :], (LOG_ROWS, WIDTH))


def summary(reverse, *arrays):
    values, proj, log_rows = [pltpu.with_memory_space_constraint(array, pltpu.HBM) for array in arrays]
    tokens = values.shape[0]

    def turn(step):
        return 1 - step if reverse else step

    rows = WIDTH if reverse else WIDTH + LOG_ROWS
    packed = jax.ShapeDtypeStruct((HALF, rows, WIDTH), f32)
    packed_spec = pl.BlockSpec((HALF, rows, WIDTH), lambda s: (0, 0, 0))
    shapes = [
        jax.ShapeDtypeStruct((HEADS, tokens, WIDTH), bf16),
        packed,
        packed,
        jax.ShapeDtypeStruct((HEADS, WIDTH, WIDTH), f32),
    ]
    specs = [
        pl.BlockSpec((HEADS, SPAN, WIDTH), lambda s: (0, turn(s), 0)),
        packed_spec,
        packed_spec,
        pl.BlockSpec((HEADS, WIDTH, WIDTH), lambda s: (0, 0, 0)),
    ]
    if not reverse:
        shapes += [
            jax.ShapeDtypeStruct((tokens, HEADS), f32),
            jax.ShapeDtypeStruct((HEADS, tokens), f32),
        ]
        specs += [
            pl.BlockSpec((SPAN, HEADS), lambda s: (turn(s), 0)),
            pl.BlockSpec((HEADS, SPAN), lambda s: (0, turn(s))),
        ]
    return pl.pallas_call(
        functools.partial(summary_body, reverse),
        grid=(2,),
        in_specs=[
            pl.BlockSpec((SPAN, HEADS, WIDTH), lambda s: (turn(s), 0, 0)),
            pl.BlockSpec((SPAN, WIDTH), lambda s: (turn(s), 0)),
            pl.BlockSpec((HEADS, tokens), lambda s: (0, 0)),
        ],
        out_specs=specs,
        out_shape=shapes,
        scratch_shapes=[pltpu.VMEM((2, HEADS, WIDTH, WIDTH), f32)],
        compiler_params=params(),
        name="summary_b" if reverse else "summary_f",
    )(values, proj, log_rows)


def line_sums(product, head):
    row = lax.broadcasted_iota(jnp.int32, (2 * WIDTH, WIDTH), 1)
    picked = jnp.where(row == head, 1.0, 0.0).astype(bf16)
    return dot(jnp.concatenate(split_two(product), axis=1), picked, ((1,), (0,)))


def intra_body(x_ref, dy_ref, b_ref, c_ref, lev_ref, lev_rows_ref, gain_ref, *refs):
    y_out, dx_out, x_t_out, dy_t_out, cross_out, grads_out = refs[-6:]
    b = b_ref[...]
    c = c_ref[...]
    low, high = slice(0, 128), slice(128, 256)
    blocks = ((low, low), (high, low), (high, high))
    scores = [dot(c[t], b[s], ((1,), (1,))) for t, s in blocks]
    row = lax.broadcasted_iota(jnp.int32, (128, 128), 0)
    column = lax.broadcasted_iota(jnp.int32, (128, 128), 1)
    causal = column <= row
    score_grad = [jnp.zeros((128, 128), f32) for _ in blocks]
    cross = jnp.zeros((SPAN, WIDTH), f32)
    for head in range(HEADS):
        x = x_ref[head]
        dy = dy_ref[head]
        gain = gain_ref[:, head : head + 1]
        level = lev_ref[:, head : head + 1]
        level_row = lev_rows_ref[head : head + 1, :]
        mixing = []
        for at, (t, s) in enumerate(blocks):
            distance = level[t] - level_row[:, s]
            if t == s:
                distance = jnp.where(causal, distance, -1e30)
            decay = jnp.exp(distance)
            mixing.append((scores[at] * decay).astype(bf16))
            score_grad[at] = score_grad[at] + decay * dot(dy[t], x[s], ((1,), (1,)))
        lower = jnp.concatenate(mixing[1:], axis=1)
        left = jnp.concatenate(mixing[:2], axis=0)
        y = jnp.concatenate([dot(mixing[0], x[low], ((1,), (0,))), dot(lower, x, ((1,), (0,)))], axis=0)
        dx = jnp.concatenate([dot(left, dy, ((0,), (0,))), dot(mixing[2], dy[high], ((0,), (0,)))], axis=0)
        x32 = x.astype(f32)
        dy32 = dy.astype(f32)
        cross = cross + line_sums(y * dy32 - dx * x32, head)
        x_t_out[head] = jnp.transpose(x)
        dy_t_out[head] = jnp.transpose(dy)
        y_out[head] = y + gain * x32
        dx_out[head] = dx + gain * dy32
    cross_out[...] = cross[:, :HEADS]
    g00, g10, g11 = [split_two(g) for g in score_grad]
    grad_c0 = sum(dot(g, b[low], ((1,), (0,))) for g in g00)
    grad_c1 = sum(dot(g, b[low], ((1,), (0,))) for g in g10) + sum(dot(g, b[high], ((1,), (0,))) for g in g11)
    grad_b0 = sum(dot(g, c[low], ((0,), (0,))) for g in g00) + sum(dot(g, c[high], ((0,), (0,))) for g in g10)
    grad_b1 = sum(dot(g, c[high], ((0,), (0,))) for g in g11)
    grads_out[:WIDTH, low] = jnp.transpose(grad_c0)
    grads_out[:WIDTH, high] = jnp.transpose(grad_c1)
    grads_out[WIDTH:, low] = jnp.transpose(grad_b0)
    grads_out[WIDTH:, high] = jnp.transpose(grad_b1)


def intra(span, x_heads, dy_heads, b_proj, c_proj, levels, level_rows, gain, after, so_far=()):
    tokens = x_heads.shape[1]
    by_head = pl.BlockSpec((HEADS, SPAN, WIDTH), lambda s: (0, span, 0))
    flat = pl.BlockSpec((SPAN, WIDTH), lambda s: (span, 0))
    thin = pl.BlockSpec((SPAN, HEADS), lambda s: (span, 0))
    turned = pl.BlockSpec((HEADS, WIDTH, SPAN), lambda s: (0, 0, span))
    turned_shape = jax.ShapeDtypeStruct((HEADS, WIDTH, tokens), bf16)
    return pl.pallas_call(
        intra_body,
        grid=(1,),
        in_specs=[
            by_head,
            by_head,
            flat,
            flat,
            thin,
            pl.BlockSpec((HEADS, SPAN), lambda s: (0, span)),
            pl.BlockSpec((1, HEADS), lambda s: (0, 0)),
            anywhere,
        ]
        + [anywhere] * len(so_far),
        out_specs=[by_head, by_head, turned, turned, thin, pl.BlockSpec((2 * WIDTH, SPAN), lambda s: (0, span))],
        out_shape=[
            jax.ShapeDtypeStruct((HEADS, tokens, WIDTH), f32),
            jax.ShapeDtypeStruct((HEADS, tokens, WIDTH), f32),
            turned_shape,
            turned_shape,
            jax.ShapeDtypeStruct((tokens, HEADS), f32),
            jax.ShapeDtypeStruct((2 * WIDTH, tokens), f32),
        ],
        input_output_aliases={8 + at: at for at in range(len(so_far))},
        compiler_params=params(),
        name="intra%d" % span,
    )(x_heads, dy_heads, b_proj, c_proj, levels, level_rows, gain, after, *so_far)


def weigh(orders, logs, after, before):
    exponent = jnp.zeros_like(logs[0])
    for order, log in zip(orders, logs):
        exponent = exponent + jnp.where((order > after) & (order < before), log, 0.0)
    return jnp.exp(exponent)


def ranks(reverse, mine):
    spots = [(mine - k + 4) % 4 for k in range(4)]
    return [3 - spot for spot in spots] if reverse else spots


def whole_of(orders, logs, states):
    return sum(weigh(orders, logs, order, 4) * state for order, state in zip(orders, states))


def prefix_of(orders, logs, states, at, entering):
    out = weigh(orders, logs, -1, orders[at]) * entering
    for k in range(4):
        if k != at:
            weight = weigh(orders, logs, orders[k], orders[at])
            out = out + jnp.where(orders[k] < orders[at], weight, 0.0) * states[k]
    return out


def small(body, outs, name, *args, scratch=(), after=()):
    count = len(args)

    def with_after(*refs):
        body(*refs[:count], *refs[count + len(after) :])

    return pl.pallas_call(
        with_after,
        in_specs=[pl.BlockSpec(memory_space=pltpu.VMEM)] * count + [anywhere] * len(after),
        out_shape=[jax.ShapeDtypeStruct(shape, f32) for shape in outs],
        scratch_shapes=[pltpu.VMEM(shape, f32) for shape in scratch],
        compiler_params=params(),
        name=name,
    )(*args, *after)


def core_up_body(keep_f, other_f, keep_b, other_b, *outs):
    first = place()[0] == 0
    for head in range(HALF):
        own_log = keep_f[head, WIDTH : WIDTH + 1, :]
        other_log = other_f[head, WIDTH : WIDTH + 1, :]
        own_forward = jnp.exp(jnp.where(first, other_log, 0.0))
        other_forward = jnp.exp(jnp.where(first, 0.0, own_log))
        own_backward = jnp.exp(jnp.where(first, 0.0, other_log))
        other_backward = jnp.exp(jnp.where(first, own_log, 0.0))
        out = outs[head // 2]
        at = head % 2
        out[at, :WIDTH, :] = own_forward * keep_f[head, :WIDTH, :] + other_forward * other_f[head, :WIDTH, :]
        out[at, WIDTH : 2 * WIDTH, :] = own_backward * keep_b[head] + other_backward * other_b[head]
        out[at, 2 * WIDTH :, :] = keep_f[head, WIDTH:, :] + other_f[head, WIDTH:, :]


def chip_up_body(*refs):
    parts, outs, units = refs[:4], refs[4:8], refs[8]
    _, chip, depth = place()
    for head in range(2):
        logs = [part[head, 2 * WIDTH : 2 * WIDTH + 1, :] for part in parts]
        for way in range(2):
            orders = ranks(way == 1, chip)
            state = whole_of(orders, logs, [part[head, way * WIDTH : way * WIDTH + WIDTH, :] for part in parts])
            for side in range(2):
                units[2 * head + side, 64 * way : 64 * way + 64, :] = state[64 * side : 64 * side + 64]
        for side in range(2):
            units[2 * head + side, 128:, :] = jnp.broadcast_to(sum(logs), (LOG_ROWS, WIDTH))
    for k in range(4):
        outs[k][...] = units[(depth + k) % 4]


def depth_up_body(*refs):
    parts, out = refs[:4], refs[4]
    depth = place()[2]
    logs = [part[128:129, :] for part in parts]
    ahead = whole_of(ranks(False, depth % 4), logs, [part[:64, :] for part in parts])
    behind = whole_of(ranks(True, depth % 4), logs, [part[64:128, :] for part in parts])
    out[...] = jnp.where(depth < 4, ahead, behind)


def depth_down_body(*refs):
    parts, came, outs = refs[:4], refs[4], refs[5:]
    depth = place()[2]
    logs = [part[128:129, :] for part in parts]
    for way in range(2):
        orders = ranks(way == 1, depth % 4)
        states = [part[64 * way : 64 * way + 64, :] for part in parts]
        entering = jnp.where((depth >= 4) == (way == 0), came[...], 0.0)
        for k in range(4):
            outs[k][64 * way : 64 * way + 64, :] = prefix_of(orders, logs, states, k, entering)


def chip_down_body(*refs):
    parts, pieces, outs, units = refs[:4], refs[4:8], refs[8:12], refs[12]
    _, chip, depth = place()
    for k in range(4):
        units[(depth + k) % 4] = pieces[k][...]
    for head in range(2):
        logs = [part[head, 2 * WIDTH : 2 * WIDTH + 1, :] for part in parts]
        for way in range(2):
            orders = ranks(way == 1, chip)
            rows = slice(way * WIDTH, way * WIDTH + WIDTH)
            entering = jnp.concatenate(
                [units[2 * head + side, 64 * way : 64 * way + 64, :] for side in range(2)], axis=0
            )
            states = [part[head, rows, :] for part in parts]
            for k in range(4):
                outs[k][head, rows, :] = prefix_of(orders, logs, states, k, entering)


def core_down_body(keep_f, other_f, keep_b, other_b, *refs):
    pieces, mine, theirs = refs[:4], refs[4], refs[5]
    first = place()[0] == 0
    for head in range(HALF):
        forward = pieces[head // 2][head % 2, :WIDTH, :]
        backward = pieces[head // 2][head % 2, WIDTH:, :]
        own_decay = jnp.exp(keep_f[head, WIDTH : WIDTH + 1, :])
        other_decay = jnp.exp(other_f[head, WIDTH : WIDTH + 1, :])
        mine[head, :WIDTH, :] = jnp.where(first, forward, other_decay * forward + other_f[head, :WIDTH, :])
        mine[head, WIDTH:, :] = jnp.where(first, other_decay * backward + other_b[head], backward)
        theirs[head, :WIDTH, :] = jnp.where(first, own_decay * forward + keep_f[head, :WIDTH, :], forward)
        theirs[head, WIDTH:, :] = jnp.where(first, backward, own_decay * backward + keep_b[head])


def over_ctx(array, target):
    return lax.ppermute(array, "ctx", [(i, target(i)) for i in range(64)])


def swap_cores(array):
    return over_ctx(array, lambda i: i ^ 1)


def along_x(array, k):
    return over_ctx(array, lambda i: i // 8 * 8 + (i // 2 + k) % 4 * 2 + i % 2)


def along_z(array, k):
    return over_ctx(array, lambda i: i // 32 * 32 + (i // 8 + k) % 4 * 8 + i % 8)


def across_z(array):
    return over_ctx(array, lambda i: i ^ 32)


def spread(parts, move, sign):
    return [parts[0]] + [move(parts[k], sign * k) for k in (1, 2, 3)]


def state_at(span, way, incoming, middle, crossed):
    return jnp.where(span == 1 - way, crossed * incoming + middle, incoming)


def row_weight(way, levels):
    return jnp.exp(levels[SPAN - 1 : SPAN, :] - levels) if way else jnp.exp(levels)


def half_of(own, array):
    core, _, _ = place()
    half = core if own else 1 - core
    return jnp.where(half == 0, array[:HALF], array[HALF:])


def grad_body(own, states, middle_f, middle_b, level_rows, x_turned, dy_turned, base, *refs):
    core, _, _ = place()
    half = core if own else 1 - core
    for span in range(2):
        lanes = slice(span * SPAN, span * SPAN + SPAN)
        rows = half_of(own, level_rows[:, lanes])
        for way, middle, values in ((0, middle_f, dy_turned), (1, middle_b, x_turned)):
            weight = jnp.exp(rows[:, SPAN - 1 : SPAN] - rows) if way else jnp.exp(rows)
            last = 2 * SPAN - 1 if way else SPAN - 1
            crossed = half_of(own, jnp.exp(level_rows[:, last : last + 1]))
            of_way = slice(way * WIDTH, way * WIDTH + WIDTH)
            acc = base[of_way, lanes]
            for at in range(HALF):
                head = half * HALF + at
                state = states[slot_of(at), of_way, :]
                if span == 1 - way:
                    state = crossed[at : at + 1, :] * state + middle[head]
                value = values[head, :, lanes]
                line = dot(
                    jnp.concatenate(split_two(state), axis=1),
                    jnp.concatenate([value, value], axis=0),
                    ((1,), (0,)),
                )
                acc = acc + weight[at : at + 1, :] * line
            if own:
                refs[0][of_way, lanes] = acc
            else:
                refs[4][lanes, of_way] = jnp.transpose(acc)
    if not own:
        mine_tp = lax.axis_index("tp")
        for k in range(4):
            start = pl.multiple_of((mine_tp + k) % 4 * 128, 128)
            refs[k][...] = refs[4][pl.ds(start, 128), :]


def grad_call(own, states, middle_f, middle_b, level_rows, x_turned, dy_turned, base):
    tokens = base.shape[1]
    outs = [base.shape] if own else [(tokens // 4, 2 * WIDTH)] * 4
    return small(
        functools.partial(grad_body, own),
        outs,
        "grads_own" if own else "grads_other",
        states,
        middle_f,
        middle_b,
        level_rows,
        x_turned,
        dy_turned,
        base,
        scratch=[] if own else [(tokens, 2 * WIDTH)],
    )


def value_body(way, got, mine, middle, levels_all, levels_ref, proj, part, values, _, out, cross_out, wide):
    core, _, _ = place()
    span = pl.program_id(0)
    weight = row_weight(way, levels_ref[...])
    row = 2 * SPAN - 1 if way else SPAN - 1
    crossed = jnp.exp(levels_all[row : row + 1, :])
    doubled = jnp.concatenate([proj[...], proj[...]], axis=1)
    cross = jnp.zeros((SPAN, WIDTH), f32)
    rows = slice(way * WIDTH, way * WIDTH + WIDTH)
    for head in range(HEADS):
        slot = slot_of(head)
        incoming = jnp.where(head // HALF == core, mine[slot, rows, :], got[slot, rows, :])
        state = state_at(span, way, incoming, middle[head], crossed[:, head : head + 1])
        far = dot(doubled, jnp.concatenate(split_two(state), axis=0), ((1,), (0,)))
        far = far * weight[:, head : head + 1]
        cross = cross + line_sums(far * values[head].astype(f32), head)
        wide[head] = (part[head] + far).astype(bf16)
    out[...] = jnp.swapaxes(wide[...], 0, 1)
    cross_out[...] = cross[:, :HEADS]


def value_call(way, got, mine, middle, levels, proj, part, values, after):
    tokens = levels.shape[0]
    states = pl.BlockSpec((HALF, 2 * WIDTH, WIDTH), lambda s: (0, 0, 0))
    by_head = pl.BlockSpec((HEADS, SPAN, WIDTH), lambda s: (0, s, 0))
    thin = pl.BlockSpec((SPAN, HEADS), lambda s: (s, 0))
    return pl.pallas_call(
        functools.partial(value_body, way),
        grid=(2,),
        in_specs=[
            states,
            states,
            pl.BlockSpec((HEADS, WIDTH, WIDTH), lambda s: (0, 0, 0)),
            pl.BlockSpec((tokens, HEADS), lambda s: (0, 0)),
            thin,
            pl.BlockSpec((SPAN, WIDTH), lambda s: (s, 0)),
            by_head,
            by_head,
            anywhere,
        ],
        out_specs=[pl.BlockSpec((SPAN, HEADS, WIDTH), lambda s: (s, 0, 0)), thin],
        out_shape=[
            jax.ShapeDtypeStruct((tokens, HEADS, WIDTH), bf16),
            jax.ShapeDtypeStruct((tokens, HEADS), f32),
        ],
        scratch_shapes=[pltpu.VMEM((HEADS, SPAN, WIDTH), bf16)],
        compiler_params=params(),
        name="values_b" if way else "values_f",
    )(got, mine, middle, levels, levels, proj, part, values, after)


def decay_body(near, forward, backward, got, mine, send_b, keep_b, level_rows, out, done):
    core, _, _ = place()
    sublane = lax.broadcasted_iota(jnp.int32, (HEADS, 1), 0)
    start = jnp.zeros((HEADS, 1), f32)
    all_log = level_rows[:, SPAN - 1 : SPAN] + level_rows[:, 2 * SPAN - 1 : 2 * SPAN]
    for head in range(HEADS):
        slot = slot_of(head)
        own = head // HALF == core
        incoming = jnp.where(own, mine[slot], got[slot])
        local = jnp.where(own, keep_b[slot], send_b[slot])
        pulled = local + jnp.exp(all_log[head : head + 1, :]) * incoming[WIDTH:]
        line = jnp.sum(jnp.sum(incoming[:WIDTH] * pulled, axis=0, keepdims=True), axis=1, keepdims=True)
        start = jnp.where(sublane == head, line, start)
    for span in range(2):
        rows = slice(span * SPAN, span * SPAN + SPAN)
        cross = jnp.transpose(near[rows, :] + forward[rows, :] - backward[rows, :])
        out[:, rows] = start - running_sum(cross, True)
        start = start - jnp.sum(cross, axis=1, keepdims=True)
    done[...] = jnp.zeros_like(done)


def over_tp(array, k):
    return lax.ppermute(array, "tp", [(i, (i + k) % 4) for i in range(4)])


def add_body(p0, p1, p2, p3, out):
    out[...] = p0[...] + p1[...] + p2[...] + p3[...]


def join_body(p0, p1, p2, p3, c_out, b_out):
    mine = lax.axis_index("tp")
    for k, piece in enumerate((p0, p1, p2, p3)):
        rows = pl.ds(pl.multiple_of((mine - k + 4) % 4 * 128, 128), 128)
        c_out[rows, :] = piece[:, :WIDTH]
        b_out[rows, :] = piece[:, WIDTH:]


def on_device(inputs, b_proj, c_proj, logdecay, skip_gain, grad_out):
    tokens = inputs.shape[0]
    log_rows = logdecay.T
    gain = skip_gain.reshape(1, HEADS)
    x_heads, send_f, keep_f, middle_f, levels, level_rows = summary(False, inputs, b_proj, log_rows)
    other_f = swap_cores(send_f)
    dy_heads, send_b, keep_b, middle_b = summary(True, grad_out, c_proj, log_rows)
    other_b = swap_cores(send_b)

    chips = small(core_up_body, [(2, TALL, WIDTH)] * 4, "core_up", keep_f, other_f, keep_b, other_b)
    local = (x_heads, dy_heads, b_proj, c_proj, levels, level_rows, gain)
    first = intra(0, *local, chips[0])
    chips = spread(chips, along_x, 1)
    unit = (WIDTH + LOG_ROWS, WIDTH)
    units = small(chip_up_body, [unit] * 4, "chip_up", *chips, scratch=[(4,) + unit], after=[first[-1]])
    units = spread(units, along_z, 1)
    (quad,) = small(depth_up_body, [(64, WIDTH)], "depth_up", *units)
    quad = across_z(quad)
    back = small(depth_down_body, [(WIDTH, WIDTH)] * 4, "depth_down", *units, quad)
    back = spread(back, along_z, -1)
    entering = small(
        chip_down_body, [(2, 2 * WIDTH, WIDTH)] * 4, "chip_down", *chips, *back, scratch=[(4, WIDTH, WIDTH)]
    )
    y_part, dx_part, x_turned, dy_turned, near, base = intra(1, *local, entering[0], first)
    entering = spread(entering, along_x, -1)
    mine, theirs = small(
        core_down_body,
        [(HALF, 2 * WIDTH, WIDTH)] * 2,
        "core_down",
        keep_f,
        other_f,
        keep_b,
        other_b,
        *entering,
        after=[base],
    )
    got = swap_cores(theirs)

    (base,) = grad_call(True, mine, middle_f, middle_b, level_rows, x_turned, dy_turned, base)
    pieces = grad_call(False, got, middle_f, middle_b, level_rows, x_turned, dy_turned, base)
    outputs, cross_f = value_call(0, got, mine, middle_f, levels, c_proj, y_part, dy_heads, pieces[0])
    pieces = spread(pieces, over_tp, 1)
    (summed,) = small(add_body, [pieces[0].shape], "add", *pieces, after=[cross_f])
    grad_inputs, cross_b = value_call(1, got, mine, middle_b, levels, b_proj, dx_part, x_heads, summed)
    decays, done = small(
        decay_body,
        [(HEADS, tokens), (8, WIDTH)],
        "decay",
        near,
        cross_f,
        cross_b,
        got,
        mine,
        send_b,
        keep_b,
        level_rows,
    )
    joined = [summed] + [over_tp(summed, k) for k in (1, 2, 3)]
    grad_c, grad_b = small(join_body, [(tokens, WIDTH)] * 2, "join", *joined, after=[done])
    return outputs, grad_inputs, decays.T, grad_b, grad_c


def solution(mesh):
    placed = (
        P("ctx", "tp", None),
        P("ctx", None),
        P("ctx", None),
        P("ctx", "tp"),
        P("tp"),
        P("ctx", "tp", None),
    )
    return jax.shard_map(
        on_device,
        mesh=mesh,
        in_specs=placed,
        out_specs=(
            P("ctx", "tp", None),
            P("ctx", "tp", None),
            P("ctx", "tp"),
            P("ctx", None),
            P("ctx", None),
        ),
        check_vma=False,
    )
```

```python
import functools

import jax
import jax.numpy as jnp
from jax import lax
from jax.experimental import pallas as pl
from jax.experimental.pallas import tpu as pltpu
from jax.sharding import PartitionSpec as P

SPAN = 256
HEADS = 16
HALF = 8
WIDTH = 128
CHIPS = 4
QUAD = 4
LOG_ROWS = 8
f32 = jnp.float32
bf16 = jnp.bfloat16
TALL = 2 * WIDTH + LOG_ROWS
anywhere = pl.BlockSpec(memory_space=pl.ANY)


def params():
    return pltpu.CompilerParams(vmem_limit_bytes=24 * 1024 * 1024)


def place():
    position = lax.axis_index("ctx")
    return position % 2, position // 2 % 4, position // 8


def dot(a, b, dims):
    return lax.dot_general(a, b, (dims, ((), ())), preferred_element_type=f32)


def split_two(a):
    high = a.astype(bf16)
    return high, (a - high.astype(f32)).astype(bf16)


def split_three(a):
    high = a.astype(bf16)
    rest = a - high.astype(f32)
    middle = rest.astype(bf16)
    return high, middle, (rest - middle.astype(f32)).astype(bf16)


def triangle(strict):
    row = lax.broadcasted_iota(jnp.int32, (SPAN, SPAN), 0)
    column = lax.broadcasted_iota(jnp.int32, (SPAN, SPAN), 1)
    kept = column < row if strict else column <= row
    return jnp.where(kept, 1.0, 0.0).astype(bf16)


def running_sum(rows, strict):
    tri = triangle(strict)
    return sum(dot(part, tri, ((1,), (1,))) for part in split_three(rows))


def kept_half():
    core, _, depth = place()
    return jnp.bitwise_xor(core, depth % 2)


def summary_body(reverse, *refs):
    if reverse:
        here, proj, rows_all, heads_out, send, keep, middle, total = refs
        order = (1, 0)
    else:
        values, proj_far, log_rows, heads_out, send, keep, middle, levels_out, rows_all, here, proj, logs, total, arrived = refs
        order = (0, 1)
        copies = [
            pltpu.make_async_copy(log_rows, logs, arrived.at[0]),
            pltpu.make_async_copy(proj_far, proj, arrived.at[1]),
        ]
        copies += [
            pltpu.make_async_copy(values.at[pl.ds(span * SPAN, SPAN)], here.at[span], arrived.at[2 + span])
            for span in order
        ]
        for copy in copies:
            copy.start()
        copies[0].wait()
        for span in order:
            tokens = slice(span * SPAN, span * SPAN + SPAN)
            level_rows = running_sum(logs[:, tokens], False)
            levels_out[tokens, :] = jnp.transpose(level_rows)
            rows_all[:, tokens] = level_rows
        copies[1].wait()
    last = [rows_all[:, SPAN * span + SPAN - 1 : SPAN * span + SPAN] for span in (0, 1)]
    carried = jnp.exp(last[order[1]])
    all_log = last[0] + last[1]
    for span in order:
        tokens = slice(span * SPAN, span * SPAN + SPAN)
        level_rows = rows_all[:, tokens]
        weight = jnp.exp(level_rows) if reverse else jnp.exp(last[span] - level_rows)
        proj_t = jnp.transpose(proj[tokens, :]).astype(f32)
        if reverse:
            swapped = jnp.swapaxes(here[tokens], 0, 1)
        else:
            copies[2 + span].wait()
            swapped = jnp.swapaxes(here[span], 0, 1)
        heads_out[:, tokens, :] = swapped
        for head in range(HEADS):
            weighted = jnp.concatenate(split_two(proj_t * weight[head : head + 1, :]), axis=0)
            both = dot(weighted, swapped[head], ((1,), (0,)))
            fresh = both[:WIDTH] + both[WIDTH:]
            if span == order[0]:
                middle[head] = fresh
            else:
                total[head] = fresh + carried[head : head + 1, :] * middle[head]
    kept = kept_half()
    for value in (0, 1):

        @pl.when(kept == value)
        def _():
            for out, half in ((keep, value), (send, 1 - value)):
                for at in range(HALF):
                    head = half * HALF + at
                    out[at, :WIDTH, :] = total[head]
                    if not reverse:
                        out[at, WIDTH:, :] = jnp.broadcast_to(all_log[head : head + 1, :], (LOG_ROWS, WIDTH))


def summary(reverse, values, proj, row_values):
    tokens = values.shape[0]
    rows = WIDTH if reverse else WIDTH + LOG_ROWS
    shapes = [
        jax.ShapeDtypeStruct((HEADS, tokens, WIDTH), bf16),
        jax.ShapeDtypeStruct((HALF, rows, WIDTH), f32),
        jax.ShapeDtypeStruct((HALF, rows, WIDTH), f32),
        jax.ShapeDtypeStruct((HEADS, WIDTH, WIDTH), f32),
    ]
    scratch = [pltpu.VMEM((HEADS, WIDTH, WIDTH), f32)]
    arrays = [values, proj, row_values]
    if not reverse:
        shapes += [
            jax.ShapeDtypeStruct((tokens, HEADS), f32),
            jax.ShapeDtypeStruct((HEADS, tokens), f32),
        ]
        scratch = [
            pltpu.VMEM((2, SPAN, HEADS, WIDTH), bf16),
            pltpu.VMEM((tokens, WIDTH), bf16),
            pltpu.VMEM((HEADS, tokens), f32),
            *scratch,
            pltpu.SemaphoreType.DMA((4,)),
        ]
        arrays = [pltpu.with_memory_space_constraint(array, pltpu.HBM) for array in arrays]
    return pl.pallas_call(
        functools.partial(summary_body, reverse),
        in_specs=[pl.BlockSpec(memory_space=pltpu.VMEM) if reverse else anywhere] * 3,
        out_shape=shapes,
        scratch_shapes=scratch,
        compiler_params=params(),
        name="summary_b" if reverse else "summary_f",
    )(*arrays)


def line_sums(product, head):
    row = lax.broadcasted_iota(jnp.int32, (2 * WIDTH, WIDTH), 1)
    picked = jnp.where(row == head, 1.0, 0.0).astype(bf16)
    return dot(jnp.concatenate(split_two(product), axis=1), picked, ((1,), (0,)))


def intra_body(x_ref, dy_ref, b_ref, c_ref, lev_ref, lev_rows_ref, gain_ref, *refs):
    y_out, dx_out, x_t_out, dy_t_out, cross_out, grads_out = refs[-6:]
    b = b_ref[...]
    c = c_ref[...]
    low, high = slice(0, 128), slice(128, 256)
    blocks = ((low, low), (high, low), (high, high))
    scores = [dot(c[t], b[s], ((1,), (1,))) for t, s in blocks]
    row = lax.broadcasted_iota(jnp.int32, (128, 128), 0)
    column = lax.broadcasted_iota(jnp.int32, (128, 128), 1)
    causal = column <= row
    score_grad = [jnp.zeros((128, 128), f32) for _ in blocks]
    cross = jnp.zeros((SPAN, WIDTH), f32)
    for head in range(HEADS):
        x = x_ref[head]
        dy = dy_ref[head]
        gain = gain_ref[:, head : head + 1]
        level = lev_ref[:, head : head + 1]
        level_row = lev_rows_ref[head : head + 1, :]
        mixing = []
        for at, (t, s) in enumerate(blocks):
            distance = level[t] - level_row[:, s]
            if t == s:
                distance = jnp.where(causal, distance, -1e30)
            decay = jnp.exp(distance)
            mixing.append((scores[at] * decay).astype(bf16))
            score_grad[at] = score_grad[at] + decay * dot(dy[t], x[s], ((1,), (1,)))
        lower = jnp.concatenate(mixing[1:], axis=1)
        left = jnp.concatenate(mixing[:2], axis=0)
        y = jnp.concatenate([dot(mixing[0], x[low], ((1,), (0,))), dot(lower, x, ((1,), (0,)))], axis=0)
        dx = jnp.concatenate([dot(left, dy, ((0,), (0,))), dot(mixing[2], dy[high], ((0,), (0,)))], axis=0)
        x32 = x.astype(f32)
        dy32 = dy.astype(f32)
        cross = cross + line_sums(y * dy32 - dx * x32, head)
        x_t_out[head] = jnp.transpose(x)
        dy_t_out[head] = jnp.transpose(dy)
        y_out[head] = y + gain * x32
        dx_out[head] = dx + gain * dy32
    cross_out[...] = cross[:, :HEADS]
    g00, g10, g11 = [split_two(g) for g in score_grad]
    grad_c0 = sum(dot(g, b[low], ((1,), (0,))) for g in g00)
    grad_c1 = sum(dot(g, b[low], ((1,), (0,))) for g in g10) + sum(dot(g, b[high], ((1,), (0,))) for g in g11)
    grad_b0 = sum(dot(g, c[low], ((0,), (0,))) for g in g00) + sum(dot(g, c[high], ((0,), (0,))) for g in g10)
    grad_b1 = sum(dot(g, c[high], ((0,), (0,))) for g in g11)
    grads_out[:WIDTH, low] = jnp.transpose(grad_c0)
    grads_out[:WIDTH, high] = jnp.transpose(grad_c1)
    grads_out[WIDTH:, low] = jnp.transpose(grad_b0)
    grads_out[WIDTH:, high] = jnp.transpose(grad_b1)


def intra(span, x_heads, dy_heads, b_proj, c_proj, levels, level_rows, gain, after, so_far=()):
    tokens = x_heads.shape[1]
    by_head = pl.BlockSpec((HEADS, SPAN, WIDTH), lambda s: (0, span, 0))
    flat = pl.BlockSpec((SPAN, WIDTH), lambda s: (span, 0))
    thin = pl.BlockSpec((SPAN, HEADS), lambda s: (span, 0))
    turned = pl.BlockSpec((HEADS, WIDTH, SPAN), lambda s: (0, 0, span))
    turned_shape = jax.ShapeDtypeStruct((HEADS, WIDTH, tokens), bf16)
    return pl.pallas_call(
        intra_body,
        grid=(1,),
        in_specs=[
            by_head,
            by_head,
            flat,
            flat,
            thin,
            pl.BlockSpec((HEADS, SPAN), lambda s: (0, span)),
            pl.BlockSpec((1, HEADS), lambda s: (0, 0)),
            anywhere,
        ]
        + [anywhere] * len(so_far),
        out_specs=[by_head, by_head, turned, turned, thin, pl.BlockSpec((2 * WIDTH, SPAN), lambda s: (0, span))],
        out_shape=[
            jax.ShapeDtypeStruct((HEADS, tokens, WIDTH), f32),
            jax.ShapeDtypeStruct((HEADS, tokens, WIDTH), f32),
            turned_shape,
            turned_shape,
            jax.ShapeDtypeStruct((tokens, HEADS), f32),
            jax.ShapeDtypeStruct((2 * WIDTH, tokens), f32),
        ],
        input_output_aliases={8 + at: at for at in range(len(so_far))},
        compiler_params=params(),
        name="intra%d" % span,
    )(x_heads, dy_heads, b_proj, c_proj, levels, level_rows, gain, after, *so_far)


def small(body, outs, name, *args, scratch=(), after=()):
    count = len(args)

    def with_after(*refs):
        body(*refs[:count], *refs[count + len(after) :])

    return pl.pallas_call(
        with_after,
        in_specs=[pl.BlockSpec(memory_space=pltpu.VMEM)] * count + [anywhere] * len(after),
        out_shape=[jax.ShapeDtypeStruct(shape, f32) for shape in outs],
        scratch_shapes=[pltpu.VMEM(shape, f32) for shape in scratch],
        compiler_params=params(),
        name=name,
    )(*args, *after)


FORWARD = slice(0, WIDTH)
BACKWARD = slice(WIDTH, 2 * WIDTH)
LOGS = slice(2 * WIDTH, TALL)


def core_up_body(keep_f, other_f, keep_b, other_b, *outs):
    core, chip, _ = place()
    first = core == 0
    for k in range(CHIPS):
        for at in range(2):
            head = jnp.bitwise_xor(chip, k) * 2 + at
            own_log = keep_f[head, WIDTH:, :]
            other_log = other_f[head, WIDTH:, :]
            own_decay = jnp.exp(own_log)[:1]
            other_decay = jnp.exp(other_log)[:1]
            own_forward = jnp.where(first, other_decay, 1.0)
            other_forward = jnp.where(first, 1.0, own_decay)
            own_backward = jnp.where(first, 1.0, other_decay)
            other_backward = jnp.where(first, own_decay, 1.0)
            outs[k][at, FORWARD, :] = own_forward * keep_f[head, :WIDTH, :] + other_forward * other_f[head, :WIDTH, :]
            outs[k][at, BACKWARD, :] = own_backward * keep_b[head] + other_backward * other_b[head]
            outs[k][at, LOGS, :] = own_log + other_log


def chain(places, decays, states, entering):
    befores = {}
    for at in places:
        befores[at] = entering
        entering = decays[at] * entering + states(at)
    return befores, entering


TAKEN = (2, 1, 3, 0)


def taken(parts):
    return [parts[k] for k in TAKEN]


def untaken(parts):
    return [parts[TAKEN.index(k)] for k in range(4)]


def slab_up_body(*refs):
    parts, out, ordered = untaken(refs[:4]), refs[4], refs[5]
    _, chip, _ = place()
    zero = jnp.zeros((WIDTH, WIDTH), f32)
    for k in range(CHIPS):
        ordered[jnp.bitwise_xor(chip, k)] = parts[k][...]
    for head in range(2):
        logs = [ordered[at, head, LOGS, :] for at in range(CHIPS)]
        decays = [jnp.exp(log)[:1] for log in logs]
        out[head, FORWARD, :] = chain(range(4), decays, lambda at: ordered[at, head, FORWARD, :], zero)[1]
        out[head, BACKWARD, :] = chain(range(3, -1, -1), decays, lambda at: ordered[at, head, BACKWARD, :], zero)[1]
        out[head, LOGS, :] = sum(logs)


def in_slab_order(own, other):
    kept = kept_half()
    return jnp.where(kept == 0, own, other), jnp.where(kept == 0, other, own)


def block_up_body(own, other, both, single):
    core, _, depth = place()
    block = depth // 2
    near = jnp.bitwise_xor(block, jnp.where(core == 0, 1, 3))
    far = jnp.bitwise_xor(block, 2)
    for head in range(2):
        log0, log1 = in_slab_order(own[head, LOGS, :], other[head, LOGS, :])
        ahead0, ahead1 = in_slab_order(own[head, FORWARD, :], other[head, FORWARD, :])
        behind0, behind1 = in_slab_order(own[head, BACKWARD, :], other[head, BACKWARD, :])
        ahead = jnp.exp(log1)[:1] * ahead0 + ahead1
        behind = behind0 + jnp.exp(log0)[:1] * behind1
        both[head, :WIDTH, :] = jnp.where(near > block, ahead, behind)
        both[head, WIDTH:, :] = log0 + log1

        @pl.when(core == head)
        def _():
            single[:WIDTH, :] = jnp.where(far > block, ahead, behind)
            single[WIDTH:, :] = log0 + log1


def chip_down_body(*refs):
    parts, (own, other, single, both, other_single, other_both) = untaken(refs[:4]), refs[4:10]
    outs, ordered, came, entered = refs[10:14], *refs[14:]
    core, chip, depth = place()
    block = depth // 2
    kept = kept_half()
    for k in range(CHIPS):
        ordered[jnp.bitwise_xor(chip, k)] = parts[k][...]
    came[block] = jnp.zeros_like(came[0])
    came[jnp.bitwise_xor(block, jnp.where(core == 0, 1, 3))] = both[...]
    came[jnp.bitwise_xor(block, jnp.where(core == 0, 3, 1))] = other_both[...]
    far = jnp.bitwise_xor(block, 2)
    came[far, core] = single[...]
    came[far, 1 - core] = other_single[...]
    for head in range(2):
        decays = [jnp.exp(ordered[at, head, LOGS, :])[:1] for at in range(CHIPS)]
        for way, rows in ((0, FORWARD), (1, BACKWARD)):
            entering = jnp.zeros((WIDTH, WIDTH), f32)
            for at in range(3, -1, -1) if way else range(4):
                counts = at > block if way else at < block
                passed = jnp.exp(came[at, head, WIDTH:, :])[:1] * entering + came[at, head, :WIDTH, :]
                entering = jnp.where(counts, passed, entering)
            crossed = jnp.exp(other[head, LOGS, :])[:1] * entering + other[head, rows, :]
            entering = jnp.where(kept == 1 - way, crossed, entering)
            places = range(3, -1, -1) if way else range(4)
            befores, _ = chain(places, decays, lambda at: ordered[at, head, rows, :], entering)
            for at, before in befores.items():
                entered[at, head, rows, :] = before
    for k in range(CHIPS):
        outs[k][...] = entered[jnp.bitwise_xor(chip, k)]


def core_down_body(keep_f, other_f, keep_b, other_b, *refs):
    pieces, mine, theirs = untaken(refs[:4]), refs[4], refs[5]
    core, chip, _ = place()
    first = core == 0
    for k in range(CHIPS):
        for at in range(2):
            head = jnp.bitwise_xor(chip, k) * 2 + at
            forward = pieces[k][at, FORWARD, :]
            backward = pieces[k][at, BACKWARD, :]
            own_decay = jnp.exp(keep_f[head, WIDTH:, :])[:1]
            other_decay = jnp.exp(other_f[head, WIDTH:, :])[:1]
            mine[head, FORWARD, :] = jnp.where(first, forward, other_decay * forward + other_f[head, :WIDTH, :])
            mine[head, BACKWARD, :] = jnp.where(first, other_decay * backward + other_b[head], backward)
            theirs[head, FORWARD, :] = jnp.where(first, own_decay * forward + keep_f[head, :WIDTH, :], forward)
            theirs[head, BACKWARD, :] = jnp.where(first, backward, own_decay * backward + keep_b[head])


def over_ctx(array, target):
    return lax.ppermute(array, "ctx", [(i, target(i)) for i in range(64)])


def swap_cores(array):
    return over_ctx(array, lambda i: i ^ 1)


def along_chips(array, k):
    return over_ctx(array, lambda i: i ^ 2 * k ^ (8 if i % 2 else 0))


def to_near_blocks(array):
    return over_ctx(array, lambda i: i ^ (48 if i % 2 else 16))


def to_far_block(array):
    return over_ctx(array, lambda i: i ^ 32)


def spread(parts, move):
    return [parts[0]] + [move(parts[k], k) for k in range(1, len(parts))]


def half_of(own, array):
    half = kept_half() if own else 1 - kept_half()
    return jnp.where(half == 0, array[:HALF], array[HALF:])


def grad_body(own, states, middle_f, middle_b, level_rows, x_turned, dy_turned, base, *refs):
    half = kept_half() if own else 1 - kept_half()
    for span in range(2):
        lanes = slice(span * SPAN, span * SPAN + SPAN)
        rows = half_of(own, level_rows[:, lanes])
        for way, middle, values in ((0, middle_f, dy_turned), (1, middle_b, x_turned)):
            weight = jnp.exp(rows[:, SPAN - 1 : SPAN] - rows) if way else jnp.exp(rows)
            last = 2 * SPAN - 1 if way else SPAN - 1
            crossed = half_of(own, jnp.exp(level_rows[:, last : last + 1]))
            of_way = slice(way * WIDTH, way * WIDTH + WIDTH)
            acc = base[of_way, lanes]
            for at in range(HALF):
                head = half * HALF + at
                state = states[at, of_way, :]
                if span == 1 - way:
                    state = crossed[at : at + 1, :] * state + middle[head]
                value = values[head, :, lanes]
                line = dot(
                    jnp.concatenate(split_two(state), axis=1),
                    jnp.concatenate([value, value], axis=0),
                    ((1,), (0,)),
                )
                acc = acc + weight[at : at + 1, :] * line
            if own:
                refs[0][of_way, lanes] = acc
            else:
                refs[4][lanes, of_way] = jnp.transpose(acc)
    if not own:
        mine_tp = lax.axis_index("tp")
        for k in range(4):
            start = pl.multiple_of(jnp.bitwise_xor(mine_tp, k) * 128, 128)
            refs[k][...] = refs[4][pl.ds(start, 128), :]


def grad_call(own, states, middle_f, middle_b, level_rows, x_turned, dy_turned, base):
    tokens = base.shape[1]
    outs = [base.shape] if own else [(tokens // 4, 2 * WIDTH)] * 4
    return small(
        functools.partial(grad_body, own),
        outs,
        "grads_own" if own else "grads_other",
        states,
        middle_f,
        middle_b,
        level_rows,
        x_turned,
        dy_turned,
        base,
        scratch=[] if own else [(tokens, 2 * WIDTH)],
    )


def value_body(way, got, mine, middle, levels, proj, part, values, _, out, cross_out, wide, turned, left):
    kept = kept_half()
    states = slice(way * WIDTH, way * WIDTH + WIDTH)
    last = 2 * SPAN - 1 if way else SPAN - 1
    crossed = jnp.exp(levels[last : last + 1, :])
    copies = []
    for span in range(2):
        tokens = slice(span * SPAN, span * SPAN + SPAN)
        level = levels[tokens, :]
        weight = jnp.exp(level[SPAN - 1 : SPAN, :] - level) if way else jnp.exp(level)
        doubled = jnp.concatenate([proj[tokens, :], proj[tokens, :]], axis=1)
        cross = jnp.zeros((SPAN, WIDTH), f32)
        for head in range(HEADS):
            at = head % HALF
            state = jnp.where(head // HALF == kept, mine[at, states, :], got[at, states, :])
            if span == 1 - way:
                state = crossed[:, head : head + 1] * state + middle[head]
            far = dot(doubled, jnp.concatenate(split_two(state), axis=0), ((1,), (0,)))
            far = far * weight[:, head : head + 1]
            cross = cross + line_sums(far * values[head, tokens, :].astype(f32), head)
            wide[span, head] = (part[head, tokens, :] + far).astype(bf16)
        cross_out[tokens, :] = cross[:, :HEADS]
        turned[span] = jnp.swapaxes(wide[span], 0, 1)
        copies.append(pltpu.make_async_copy(turned.at[span], out.at[pl.ds(span * SPAN, SPAN)], left.at[span]))
        copies[-1].start()
    for copy in copies:
        copy.wait()


def value_call(way, got, mine, middle, levels, proj, part, values, after):
    tokens = levels.shape[0]
    return pl.pallas_call(
        functools.partial(value_body, way),
        in_specs=[pl.BlockSpec(memory_space=pltpu.VMEM)] * 7 + [anywhere],
        out_specs=[anywhere, pl.BlockSpec(memory_space=pltpu.VMEM)],
        out_shape=[
            jax.ShapeDtypeStruct((tokens, HEADS, WIDTH), bf16),
            jax.ShapeDtypeStruct((tokens, HEADS), f32),
        ],
        scratch_shapes=[
            pltpu.VMEM((2, HEADS, SPAN, WIDTH), bf16),
            pltpu.VMEM((2, SPAN, HEADS, WIDTH), bf16),
            pltpu.SemaphoreType.DMA((2,)),
        ],
        compiler_params=params(),
        name="values_b" if way else "values_f",
    )(got, mine, middle, levels, proj, part, values, after)


def decay_body(near, forward, backward, got, mine, send_b, keep_b, level_rows, out, done):
    kept = kept_half()
    sublane = lax.broadcasted_iota(jnp.int32, (HEADS, 1), 0)
    start = jnp.zeros((HEADS, 1), f32)
    all_log = level_rows[:, SPAN - 1 : SPAN] + level_rows[:, 2 * SPAN - 1 : 2 * SPAN]
    for head in range(HEADS):
        at = head % HALF
        own = head // HALF == kept
        incoming = jnp.where(own, mine[at], got[at])
        local = jnp.where(own, keep_b[at], send_b[at])
        pulled = local + jnp.exp(all_log[head : head + 1, :]) * incoming[WIDTH:]
        line = jnp.sum(jnp.sum(incoming[:WIDTH] * pulled, axis=0, keepdims=True), axis=1, keepdims=True)
        start = jnp.where(sublane == head, line, start)
    for span in range(2):
        rows = slice(span * SPAN, span * SPAN + SPAN)
        cross = jnp.transpose(near[rows, :] + forward[rows, :] - backward[rows, :])
        out[:, rows] = start - running_sum(cross, True)
        start = start - jnp.sum(cross, axis=1, keepdims=True)
    done[...] = jnp.zeros_like(done)


def over_tp(array, k):
    return lax.ppermute(array, "tp", [(i, i ^ k) for i in range(4)])


def add_body(p2, p1, p3, p0, out):
    out[...] = p0[...] + p1[...] + p2[...] + p3[...]


def join_body(p2, p1, p3, p0, c_out, b_out):
    mine = lax.axis_index("tp")
    for k, piece in enumerate((p0, p1, p2, p3)):
        rows = pl.ds(pl.multiple_of(jnp.bitwise_xor(mine, k) * 128, 128), 128)
        c_out[rows, :] = piece[:, :WIDTH]
        b_out[rows, :] = piece[:, WIDTH:]


def on_device(inputs, b_proj, c_proj, logdecay, skip_gain, grad_out):
    tokens = inputs.shape[0]
    log_rows = logdecay.T
    gain = skip_gain.reshape(1, HEADS)
    x_heads, send_f, keep_f, middle_f, levels, level_rows = summary(False, inputs, b_proj, log_rows)
    other_f = swap_cores(send_f)
    dy_heads, send_b, keep_b, middle_b = summary(True, grad_out, c_proj, level_rows)
    other_b = swap_cores(send_b)

    cores = (keep_f, other_f, keep_b, other_b)
    packed = (2, TALL, WIDTH)
    chips = small(core_up_body, [packed] * CHIPS, "core_up", *cores)
    local = (x_heads, dy_heads, b_proj, c_proj, levels, level_rows, gain)
    first = intra(0, *local, chips[0])
    chips = [along_chips(chips[k], k) for k in range(CHIPS)]
    (slab,) = small(slab_up_body, [packed], "slab_up", *taken(chips), scratch=[(CHIPS,) + packed], after=[first[-1]])
    other_slab = swap_cores(slab)
    unit = (WIDTH + LOG_ROWS, WIDTH)
    both, single = small(block_up_body, [(2,) + unit, unit], "block_up", slab, other_slab)
    single = to_far_block(single)
    both = to_near_blocks(both)
    entering = small(
        chip_down_body,
        [(2, 2 * WIDTH, WIDTH)] * CHIPS,
        "chip_down",
        *taken(chips),
        slab,
        other_slab,
        single,
        both,
        swap_cores(single),
        swap_cores(both),
        scratch=[(CHIPS,) + packed, (4, 2) + unit, (CHIPS, 2, 2 * WIDTH, WIDTH)],
    )
    y_part, dx_part, x_turned, dy_turned, near, base = intra(1, *local, entering[0], first)
    entering = [along_chips(entering[k], k) for k in range(CHIPS)]
    mine, theirs = small(
        core_down_body, [(HALF, 2 * WIDTH, WIDTH)] * 2, "core_down", *cores, *taken(entering), after=[base]
    )
    got = swap_cores(theirs)

    (base,) = grad_call(True, mine, middle_f, middle_b, level_rows, x_turned, dy_turned, base)
    pieces = grad_call(False, got, middle_f, middle_b, level_rows, x_turned, dy_turned, base)
    outputs, cross_f = value_call(0, got, mine, middle_f, levels, c_proj, y_part, dy_heads, pieces[0])
    pieces = spread(pieces, over_tp)
    (summed,) = small(add_body, [pieces[0].shape], "add", *taken(pieces), after=[cross_f])
    grad_inputs, cross_b = value_call(1, got, mine, middle_b, levels, b_proj, dx_part, x_heads, summed)
    decays, done = small(
        decay_body,
        [(HEADS, tokens), (8, WIDTH)],
        "decay",
        near,
        cross_f,
        cross_b,
        got,
        mine,
        send_b,
        keep_b,
        level_rows,
    )
    joined = spread([summed] * 4, over_tp)
    grad_c, grad_b = small(join_body, [(tokens, WIDTH)] * 2, "join", *taken(joined), after=[done])
    return outputs, grad_inputs, decays.T, grad_b, grad_c


def solution(mesh):
    placed = (
        P("ctx", "tp", None),
        P("ctx", None),
        P("ctx", None),
        P("ctx", "tp"),
        P("tp"),
        P("ctx", "tp", None),
    )
    return jax.shard_map(
        on_device,
        mesh=mesh,
        in_specs=placed,
        out_specs=(
            P("ctx", "tp", None),
            P("ctx", "tp", None),
            P("ctx", "tp"),
            P("ctx", None),
            P("ctx", None),
        ),
        check_vma=False,
    )
```

```python
import functools

import jax
import jax.numpy as jnp
from jax import lax
from jax.experimental import pallas as pl
from jax.experimental.pallas import tpu as pltpu
from jax.sharding import PartitionSpec as P

SPAN = 256
HEADS = 16
HALF = 8
WIDTH = 128
CHIPS = 4
QUAD = 4
LOG_ROWS = 8
f32 = jnp.float32
bf16 = jnp.bfloat16
TALL = 2 * WIDTH + LOG_ROWS
anywhere = pl.BlockSpec(memory_space=pl.ANY)


def params():
    return pltpu.CompilerParams(vmem_limit_bytes=24 * 1024 * 1024)


def place():
    position = lax.axis_index("ctx")
    return position % 2, position // 2 % 4, position // 8


def dot(a, b, dims):
    return lax.dot_general(a, b, (dims, ((), ())), preferred_element_type=f32)


def split_two(a):
    high = a.astype(bf16)
    return high, (a - high.astype(f32)).astype(bf16)


def split_three(a):
    high = a.astype(bf16)
    rest = a - high.astype(f32)
    middle = rest.astype(bf16)
    return high, middle, (rest - middle.astype(f32)).astype(bf16)


def triangle(strict):
    row = lax.broadcasted_iota(jnp.int32, (SPAN, SPAN), 0)
    column = lax.broadcasted_iota(jnp.int32, (SPAN, SPAN), 1)
    kept = column < row if strict else column <= row
    return jnp.where(kept, 1.0, 0.0).astype(bf16)


def running_sum(rows, strict):
    count = rows.shape[0]
    sums = dot(jnp.concatenate(split_three(rows), axis=0), triangle(strict), ((1,), (1,)))
    return sums[:count] + sums[count : 2 * count] + sums[2 * count :]


def kept_half():
    core, _, depth = place()
    return jnp.bitwise_xor(core, depth % 2)


def fresh_state(proj_t, weight, value):
    weighted = jnp.concatenate(split_two(proj_t * weight), axis=0)
    both = dot(weighted, value, ((1,), (0,)))
    return both[:WIDTH] + both[WIDTH:]


def summary_body(values, proj_far, log_rows, *refs):
    heads_out, send, keep, middle, proj_out, levels_out, rows_all, here, proj, logs, total, arrived = refs
    copies = [
        pltpu.make_async_copy(log_rows, logs, arrived.at[0]),
        pltpu.make_async_copy(proj_far, proj, arrived.at[1]),
    ]
    copies += [
        pltpu.make_async_copy(values.at[pl.ds(span * SPAN, SPAN)], here.at[span], arrived.at[2 + span]) for span in (0, 1)
    ]
    for copy in copies:
        copy.start()
    copies[0].wait()
    sums = running_sum(jnp.concatenate([logs[:, :SPAN], logs[:, SPAN:]], axis=0), False)
    for span in (0, 1):
        tokens = slice(span * SPAN, span * SPAN + SPAN)
        level_rows = sums[span * HEADS : span * HEADS + HEADS]
        levels_out[tokens, :] = jnp.transpose(level_rows)
        rows_all[:, tokens] = level_rows
    copies[1].wait()
    last = [rows_all[:, SPAN * span + SPAN - 1 : SPAN * span + SPAN] for span in (0, 1)]
    carried = jnp.exp(last[1])
    all_log = last[0] + last[1]
    for span in (0, 1):
        tokens = slice(span * SPAN, span * SPAN + SPAN)
        weight = jnp.exp(last[span] - rows_all[:, tokens])
        proj_t = jnp.transpose(proj[tokens, :]).astype(f32)
        proj_out[:, tokens] = proj_t
        copies[2 + span].wait()
        swapped = jnp.swapaxes(here[span], 0, 1)
        heads_out[:, tokens, :] = swapped
        for head in range(HEADS):
            fresh = fresh_state(proj_t, weight[head : head + 1, :], swapped[head])
            if span == 0:
                middle[head] = fresh
            else:
                total[head] = fresh + carried[head : head + 1, :] * middle[head]
    kept = kept_half()
    for value in (0, 1):

        @pl.when(kept == value)
        def _():
            for out, half in ((keep, value), (send, 1 - value)):
                for at in range(HALF):
                    head = half * HALF + at
                    out[at, :WIDTH, :] = total[head]
                    out[at, WIDTH:, :] = jnp.broadcast_to(all_log[head : head + 1, :], (LOG_ROWS, WIDTH))


def summary(values, proj, log_rows):
    tokens = values.shape[0]
    packed = jax.ShapeDtypeStruct((HALF, WIDTH + LOG_ROWS, WIDTH), f32)
    return pl.pallas_call(
        summary_body,
        in_specs=[anywhere] * 3,
        out_shape=[
            jax.ShapeDtypeStruct((HEADS, tokens, WIDTH), bf16),
            packed,
            packed,
            jax.ShapeDtypeStruct((HEADS, WIDTH, WIDTH), f32),
            jax.ShapeDtypeStruct((WIDTH, tokens), f32),
            jax.ShapeDtypeStruct((tokens, HEADS), f32),
            jax.ShapeDtypeStruct((HEADS, tokens), f32),
        ],
        scratch_shapes=[
            pltpu.VMEM((2, SPAN, HEADS, WIDTH), bf16),
            pltpu.VMEM((tokens, WIDTH), bf16),
            pltpu.VMEM((HEADS, tokens), f32),
            pltpu.VMEM((HEADS, WIDTH, WIDTH), f32),
            pltpu.SemaphoreType.DMA((4,)),
        ],
        compiler_params=params(),
        name="summary_f",
    )(*[pltpu.with_memory_space_constraint(array, pltpu.HBM) for array in (values, proj, log_rows)])


def pulled_half(own, heads, proj_t, rows_all, middle, total):
    half = kept_half() if own else 1 - kept_half()
    rows = jnp.where(half == 0, rows_all[:HALF], rows_all[HALF:])
    carried = jnp.exp(rows[:, SPAN - 1 : SPAN])
    for span in (1, 0):
        tokens = slice(span * SPAN, span * SPAN + SPAN)
        weight = jnp.exp(rows[:, tokens])
        for at in range(HALF):
            fresh = fresh_state(proj_t[:, tokens], weight[at : at + 1, :], heads[half * HALF + at, tokens, :])
            if span == 1:
                middle[at] = fresh
            else:
                total[at] = fresh + carried[at : at + 1, :] * middle[at]


def pulled_send_body(values, proj, rows_all, heads_out, proj_out, middle, send):
    for span in (0, 1):
        tokens = slice(span * SPAN, span * SPAN + SPAN)
        proj_out[:, tokens] = jnp.transpose(proj[tokens, :]).astype(f32)
        heads_out[:, tokens, :] = jnp.swapaxes(values[tokens], 0, 1)
    pulled_half(False, heads_out, proj_out, rows_all, middle, send)


def pulled_keep_body(heads, proj_t, rows_all, middle_send, middle, keep, scratch):
    pulled_half(True, heads, proj_t, rows_all, scratch, keep)
    kept = kept_half()
    for at in range(HALF):
        middle[kept * HALF + at] = scratch[at]
        middle[(1 - kept) * HALF + at] = middle_send[at]


def pulled_send(values, proj, rows_all):
    tokens = values.shape[0]
    half = jax.ShapeDtypeStruct((HALF, WIDTH, WIDTH), f32)
    return pl.pallas_call(
        pulled_send_body,
        in_specs=[pl.BlockSpec(memory_space=pltpu.VMEM)] * 3,
        out_shape=[
            jax.ShapeDtypeStruct((HEADS, tokens, WIDTH), bf16),
            jax.ShapeDtypeStruct((WIDTH, tokens), f32),
            half,
            half,
        ],
        compiler_params=params(),
        name="summary_b_send",
    )(values, proj, rows_all)


def line_sums(product, head):
    row = lax.broadcasted_iota(jnp.int32, (2 * WIDTH, WIDTH), 1)
    picked = jnp.where(row == head, 1.0, 0.0).astype(bf16)
    return dot(jnp.concatenate(split_two(product), axis=1), picked, ((1,), (0,)))


def intra_body(x_ref, dy_ref, b_ref, c_ref, lev_ref, lev_rows_ref, gain_ref, *refs):
    y_out, dx_out, x_t_out, dy_t_out, cross_out, grads_out = refs[-6:]
    b = b_ref[...]
    c = c_ref[...]
    low, high = slice(0, 128), slice(128, 256)
    blocks = ((low, low), (high, low), (high, high))
    scores = [dot(c[t], b[s], ((1,), (1,))) for t, s in blocks]
    row = lax.broadcasted_iota(jnp.int32, (128, 128), 0)
    column = lax.broadcasted_iota(jnp.int32, (128, 128), 1)
    causal = column <= row
    score_grad = [jnp.zeros((128, 128), f32) for _ in blocks]
    cross = jnp.zeros((SPAN, WIDTH), f32)
    for head in range(HEADS):
        x = x_ref[head]
        dy = dy_ref[head]
        gain = gain_ref[:, head : head + 1]
        level = lev_ref[:, head : head + 1]
        level_row = lev_rows_ref[head : head + 1, :]
        mixing = []
        for at, (t, s) in enumerate(blocks):
            distance = level[t] - level_row[:, s]
            if t == s:
                distance = jnp.where(causal, distance, -1e30)
            decay = jnp.exp(distance)
            mixing.append((scores[at] * decay).astype(bf16))
            score_grad[at] = score_grad[at] + decay * dot(dy[t], x[s], ((1,), (1,)))
        lower = jnp.concatenate(mixing[1:], axis=1)
        left = jnp.concatenate(mixing[:2], axis=0)
        y = jnp.concatenate([dot(mixing[0], x[low], ((1,), (0,))), dot(lower, x, ((1,), (0,)))], axis=0)
        dx = jnp.concatenate([dot(left, dy, ((0,), (0,))), dot(mixing[2], dy[high], ((0,), (0,)))], axis=0)
        x32 = x.astype(f32)
        dy32 = dy.astype(f32)
        cross = cross + line_sums(y * dy32 - dx * x32, head)
        x_t_out[head] = jnp.transpose(x)
        dy_t_out[head] = jnp.transpose(dy)
        y_out[head] = y + gain * x32
        dx_out[head] = dx + gain * dy32
    cross_out[...] = jnp.transpose(cross[:, :HEADS])
    g00, g10, g11 = [split_two(g) for g in score_grad]
    grad_c0 = sum(dot(g, b[low], ((1,), (0,))) for g in g00)
    grad_c1 = sum(dot(g, b[low], ((1,), (0,))) for g in g10) + sum(dot(g, b[high], ((1,), (0,))) for g in g11)
    grad_b0 = sum(dot(g, c[low], ((0,), (0,))) for g in g00) + sum(dot(g, c[high], ((0,), (0,))) for g in g10)
    grad_b1 = sum(dot(g, c[high], ((0,), (0,))) for g in g11)
    grads_out[:WIDTH, low] = jnp.transpose(grad_c0)
    grads_out[:WIDTH, high] = jnp.transpose(grad_c1)
    grads_out[WIDTH:, low] = jnp.transpose(grad_b0)
    grads_out[WIDTH:, high] = jnp.transpose(grad_b1)


def intra(span, x_heads, dy_heads, b_proj, c_proj, levels, level_rows, gain, after, so_far=()):
    tokens = x_heads.shape[1]
    by_head = pl.BlockSpec((HEADS, SPAN, WIDTH), lambda s: (0, span, 0))
    flat = pl.BlockSpec((SPAN, WIDTH), lambda s: (span, 0))
    thin = pl.BlockSpec((SPAN, HEADS), lambda s: (span, 0))
    rows = pl.BlockSpec((HEADS, SPAN), lambda s: (0, span))
    turned = pl.BlockSpec((HEADS, WIDTH, SPAN), lambda s: (0, 0, span))
    turned_shape = jax.ShapeDtypeStruct((HEADS, WIDTH, tokens), bf16)
    return pl.pallas_call(
        intra_body,
        grid=(1,),
        in_specs=[
            by_head,
            by_head,
            flat,
            flat,
            thin,
            rows,
            pl.BlockSpec((1, HEADS), lambda s: (0, 0)),
            anywhere,
        ]
        + [anywhere] * len(so_far),
        out_specs=[by_head, by_head, turned, turned, rows, pl.BlockSpec((2 * WIDTH, SPAN), lambda s: (0, span))],
        out_shape=[
            jax.ShapeDtypeStruct((HEADS, tokens, WIDTH), f32),
            jax.ShapeDtypeStruct((HEADS, tokens, WIDTH), f32),
            turned_shape,
            turned_shape,
            jax.ShapeDtypeStruct((HEADS, tokens), f32),
            jax.ShapeDtypeStruct((2 * WIDTH, tokens), f32),
        ],
        input_output_aliases={8 + at: at for at in range(len(so_far))},
        compiler_params=params(),
        name="intra%d" % span,
    )(x_heads, dy_heads, b_proj, c_proj, levels, level_rows, gain, after, *so_far)


def small(body, outs, name, *args, scratch=(), after=()):
    count = len(args)

    def with_after(*refs):
        body(*refs[:count], *refs[count + len(after) :])

    return pl.pallas_call(
        with_after,
        in_specs=[pl.BlockSpec(memory_space=pltpu.VMEM)] * count + [anywhere] * len(after),
        out_shape=[jax.ShapeDtypeStruct(shape, f32) for shape in outs],
        scratch_shapes=[pltpu.VMEM(shape, f32) for shape in scratch],
        compiler_params=params(),
        name=name,
    )(*args, *after)


FORWARD = slice(0, WIDTH)
BACKWARD = slice(WIDTH, 2 * WIDTH)
LOGS = slice(2 * WIDTH, TALL)


def core_up_body(keep_f, other_f, keep_b, other_b, *outs):
    core, chip, _ = place()
    first = core == 0
    for k in range(CHIPS):
        for at in range(2):
            head = jnp.bitwise_xor(chip, k) * 2 + at
            own_log = keep_f[head, WIDTH:, :]
            other_log = other_f[head, WIDTH:, :]
            own_decay = jnp.exp(own_log)[:1]
            other_decay = jnp.exp(other_log)[:1]
            own_forward = jnp.where(first, other_decay, 1.0)
            other_forward = jnp.where(first, 1.0, own_decay)
            own_backward = jnp.where(first, 1.0, other_decay)
            other_backward = jnp.where(first, own_decay, 1.0)
            outs[k][at, FORWARD, :] = own_forward * keep_f[head, :WIDTH, :] + other_forward * other_f[head, :WIDTH, :]
            outs[k][at, BACKWARD, :] = own_backward * keep_b[head] + other_backward * other_b[head]
            outs[k][at, LOGS, :] = own_log + other_log


def chain(places, decays, states, entering):
    befores = {}
    for at in places:
        befores[at] = entering
        entering = decays[at] * entering + states(at)
    return befores, entering


TAKEN = (2, 1, 3, 0)


def taken(parts):
    return [parts[k] for k in TAKEN]


def untaken(parts):
    return [parts[TAKEN.index(k)] for k in range(4)]


def slab_up_body(*refs):
    parts, out, ordered = untaken(refs[:4]), refs[4], refs[5]
    _, chip, _ = place()
    zero = jnp.zeros((WIDTH, WIDTH), f32)
    for k in range(CHIPS):
        ordered[jnp.bitwise_xor(chip, k)] = parts[k][...]
    for head in range(2):
        logs = [ordered[at, head, LOGS, :] for at in range(CHIPS)]
        decays = [jnp.exp(log)[:1] for log in logs]
        out[head, FORWARD, :] = chain(range(4), decays, lambda at: ordered[at, head, FORWARD, :], zero)[1]
        out[head, BACKWARD, :] = chain(range(3, -1, -1), decays, lambda at: ordered[at, head, BACKWARD, :], zero)[1]
        out[head, LOGS, :] = sum(logs)


def in_slab_order(own, other):
    kept = kept_half()
    return jnp.where(kept == 0, own, other), jnp.where(kept == 0, other, own)


def block_up_body(own, other, both, single):
    core, _, depth = place()
    block = depth // 2
    near = jnp.bitwise_xor(block, jnp.where(core == 0, 1, 3))
    far = jnp.bitwise_xor(block, 2)
    for head in range(2):
        log0, log1 = in_slab_order(own[head, LOGS, :], other[head, LOGS, :])
        ahead0, ahead1 = in_slab_order(own[head, FORWARD, :], other[head, FORWARD, :])
        behind0, behind1 = in_slab_order(own[head, BACKWARD, :], other[head, BACKWARD, :])
        ahead = jnp.exp(log1)[:1] * ahead0 + ahead1
        behind = behind0 + jnp.exp(log0)[:1] * behind1
        both[head, :WIDTH, :] = jnp.where(near > block, ahead, behind)
        both[head, WIDTH:, :] = log0 + log1

        @pl.when(core == head)
        def _():
            single[:WIDTH, :] = jnp.where(far > block, ahead, behind)
            single[WIDTH:, :] = log0 + log1


def chip_down_body(*refs):
    parts, (own, other, single, both, other_single, other_both) = untaken(refs[:4]), refs[4:10]
    outs, ordered, came, entered = refs[10:14], *refs[14:]
    core, chip, depth = place()
    block = depth // 2
    kept = kept_half()
    for k in range(CHIPS):
        ordered[jnp.bitwise_xor(chip, k)] = parts[k][...]
    came[block] = jnp.zeros_like(came[0])
    came[jnp.bitwise_xor(block, jnp.where(core == 0, 1, 3))] = both[...]
    came[jnp.bitwise_xor(block, jnp.where(core == 0, 3, 1))] = other_both[...]
    far = jnp.bitwise_xor(block, 2)
    came[far, core] = single[...]
    came[far, 1 - core] = other_single[...]
    for head in range(2):
        decays = [jnp.exp(ordered[at, head, LOGS, :])[:1] for at in range(CHIPS)]
        for way, rows in ((0, FORWARD), (1, BACKWARD)):
            entering = jnp.zeros((WIDTH, WIDTH), f32)
            for at in range(3, -1, -1) if way else range(4):
                counts = at > block if way else at < block
                passed = jnp.exp(came[at, head, WIDTH:, :])[:1] * entering + came[at, head, :WIDTH, :]
                entering = jnp.where(counts, passed, entering)
            crossed = jnp.exp(other[head, LOGS, :])[:1] * entering + other[head, rows, :]
            entering = jnp.where(kept == 1 - way, crossed, entering)
            places = range(3, -1, -1) if way else range(4)
            befores, _ = chain(places, decays, lambda at: ordered[at, head, rows, :], entering)
            for at, before in befores.items():
                entered[at, head, rows, :] = before
    for k in range(CHIPS):
        outs[k][...] = entered[jnp.bitwise_xor(chip, k)]


def core_down_body(keep_f, other_f, keep_b, other_b, *refs):
    pieces, mine, theirs = untaken(refs[:4]), refs[4], refs[5]
    core, chip, _ = place()
    first = core == 0
    for k in range(CHIPS):
        for at in range(2):
            head = jnp.bitwise_xor(chip, k) * 2 + at
            forward = pieces[k][at, FORWARD, :]
            backward = pieces[k][at, BACKWARD, :]
            own_decay = jnp.exp(keep_f[head, WIDTH:, :])[:1]
            other_decay = jnp.exp(other_f[head, WIDTH:, :])[:1]
            mine[head, FORWARD, :] = jnp.where(first, forward, other_decay * forward + other_f[head, :WIDTH, :])
            mine[head, BACKWARD, :] = jnp.where(first, other_decay * backward + other_b[head], backward)
            theirs[head, FORWARD, :] = jnp.where(first, own_decay * forward + keep_f[head, :WIDTH, :], forward)
            theirs[head, BACKWARD, :] = jnp.where(first, backward, own_decay * backward + keep_b[head])


def over_ctx(array, target):
    return lax.ppermute(array, "ctx", [(i, target(i)) for i in range(64)])


def swap_cores(array):
    return over_ctx(array, lambda i: i ^ 1)


def along_chips(array, k):
    return over_ctx(array, lambda i: i ^ 2 * k ^ (8 if i % 2 else 0))


def to_near_blocks(array):
    return over_ctx(array, lambda i: i ^ (48 if i % 2 else 16))


def to_far_block(array):
    return over_ctx(array, lambda i: i ^ 32)


def spread(parts, move):
    return [parts[0]] + [move(parts[k], k) for k in range(1, len(parts))]


def half_of(own, array):
    half = kept_half() if own else 1 - kept_half()
    return jnp.where(half == 0, array[:HALF], array[HALF:])


def lines_of(own, span, way, states, middle, level_rows, values):
    half = kept_half() if own else 1 - kept_half()
    lanes = slice(span * SPAN, span * SPAN + SPAN)
    rows = half_of(own, level_rows[:, lanes])
    weight = jnp.exp(rows[:, SPAN - 1 : SPAN] - rows) if way else jnp.exp(rows)
    last = 2 * SPAN - 1 if way else SPAN - 1
    crossed = half_of(own, jnp.exp(level_rows[:, last : last + 1]))
    for at in range(HALF):
        head = half * HALF + at
        state = states[at, way * WIDTH : way * WIDTH + WIDTH, :]
        if span == 1 - way:
            state = crossed[at : at + 1, :] * state + middle[head]
        value = values[head, :, lanes]
        line = dot(
            jnp.concatenate(split_two(state), axis=1),
            jnp.concatenate([value, value], axis=0),
            ((1,), (0,)),
        )
        yield weight[at : at + 1, :], line


def grad_body(own, states, middle_f, middle_b, level_rows, x_turned, dy_turned, b_turned, c_turned, base, *refs):
    for span in range(2):
        lanes = slice(span * SPAN, span * SPAN + SPAN)
        crosses = []
        for way, middle, values, proj in ((0, middle_f, dy_turned, c_turned), (1, middle_b, x_turned, b_turned)):
            of_way = slice(way * WIDTH, way * WIDTH + WIDTH)
            acc = base[of_way, lanes]
            crosses.append([])
            for weight, line in lines_of(own, span, way, states, middle, level_rows, values):
                acc = acc + weight * line
                if own:
                    crosses[way].append(weight * jnp.sum(proj[:, lanes] * line, axis=0, keepdims=True))
            if own:
                refs[0][of_way, lanes] = acc
            else:
                refs[4][lanes, of_way] = jnp.transpose(acc)
        if own:
            for at in range(HALF):
                refs[1][at : at + 1, lanes] = crosses[0][at] - crosses[1][at]
    if not own:
        mine_tp = lax.axis_index("tp")
        for k in range(4):
            start = pl.multiple_of(jnp.bitwise_xor(mine_tp, k) * 128, 128)
            refs[k][...] = refs[4][pl.ds(start, 128), :]


def cross_body(states, middle_f, middle_b, level_rows, x_turned, dy_turned, b_turned, c_turned, out):
    for span in range(2):
        lanes = slice(span * SPAN, span * SPAN + SPAN)
        crosses = []
        for way, middle, values, proj in ((0, middle_f, dy_turned, c_turned), (1, middle_b, x_turned, b_turned)):
            lines = lines_of(False, span, way, states, middle, level_rows, values)
            crosses.append([weight * jnp.sum(proj[:, lanes] * line, axis=0, keepdims=True) for weight, line in lines])
        for at in range(HALF):
            out[at : at + 1, lanes] = crosses[0][at] - crosses[1][at]


def grad_call(own, states, *arrays):
    tokens = arrays[-1].shape[1]
    outs = [arrays[-1].shape, (HALF, tokens)] if own else [(tokens // 4, 2 * WIDTH)] * 4
    return small(
        functools.partial(grad_body, own),
        outs,
        "grads_own" if own else "grads_other",
        states,
        *arrays,
        scratch=[] if own else [(tokens, 2 * WIDTH)],
    )


def value_body(way, got, mine, middle, levels, proj, part, _, out, done, wide, turned, left):
    kept = kept_half()
    states = slice(way * WIDTH, way * WIDTH + WIDTH)
    last = 2 * SPAN - 1 if way else SPAN - 1
    crossed = jnp.exp(levels[last : last + 1, :])
    copies = []
    for span in range(2):
        tokens = slice(span * SPAN, span * SPAN + SPAN)
        level = levels[tokens, :]
        weight = jnp.exp(level[SPAN - 1 : SPAN, :] - level) if way else jnp.exp(level)
        doubled = jnp.concatenate([proj[tokens, :], proj[tokens, :]], axis=1)
        for head in range(HEADS):
            at = head % HALF
            state = jnp.where(head // HALF == kept, mine[at, states, :], got[at, states, :])
            if span == 1 - way:
                state = crossed[:, head : head + 1] * state + middle[head]
            far = dot(doubled, jnp.concatenate(split_two(state), axis=0), ((1,), (0,)))
            far = far * weight[:, head : head + 1]
            wide[span, head] = (part[head, tokens, :] + far).astype(bf16)
        turned[span] = jnp.swapaxes(wide[span], 0, 1)
        copies.append(pltpu.make_async_copy(turned.at[span], out.at[pl.ds(span * SPAN, SPAN)], left.at[span]))
        copies[-1].start()
    done[...] = jnp.zeros_like(done)
    for copy in copies:
        copy.wait()


def value_call(way, got, mine, middle, levels, proj, part, after):
    tokens = levels.shape[0]
    return pl.pallas_call(
        functools.partial(value_body, way),
        in_specs=[pl.BlockSpec(memory_space=pltpu.VMEM)] * 6 + [anywhere],
        out_specs=[anywhere, pl.BlockSpec(memory_space=pltpu.VMEM)],
        out_shape=[
            jax.ShapeDtypeStruct((tokens, HEADS, WIDTH), bf16),
            jax.ShapeDtypeStruct((8, WIDTH), f32),
        ],
        scratch_shapes=[
            pltpu.VMEM((2, HEADS, SPAN, WIDTH), bf16),
            pltpu.VMEM((2, SPAN, HEADS, WIDTH), bf16),
            pltpu.SemaphoreType.DMA((2,)),
        ],
        compiler_params=params(),
        name="values_b" if way else "values_f",
    )(got, mine, middle, levels, proj, part, after)


def start_body(got, mine, send_b, keep_b, level_rows, out):
    kept = kept_half()
    all_log = level_rows[:, SPAN - 1 : SPAN] + level_rows[:, 2 * SPAN - 1 : 2 * SPAN]
    for head in range(HEADS):
        at = head % HALF
        own = head // HALF == kept
        incoming = jnp.where(own, mine[at], got[at])
        local = jnp.where(own, keep_b[at], send_b[at])
        pulled = local + jnp.exp(all_log[head : head + 1, :]) * incoming[WIDTH:]
        line = jnp.sum(jnp.sum(incoming[:WIDTH] * pulled, axis=0, keepdims=True), axis=1, keepdims=True)
        out[head : head + 1, :] = jnp.broadcast_to(line, (1, WIDTH))


def decay_body(near, cross_own, cross_other, start_ref, out, done):
    kept = kept_half()
    start = start_ref[:, :1]
    for span in range(2):
        rows = slice(span * SPAN, span * SPAN + SPAN)
        own = cross_own[:, rows]
        other = cross_other[:, rows]
        far = jnp.concatenate([jnp.where(kept == 0, own, other), jnp.where(kept == 0, other, own)], axis=0)
        cross = near[:, rows] + far
        out[:, rows] = start - running_sum(cross, True)
        start = start - jnp.sum(cross, axis=1, keepdims=True)
    done[...] = jnp.zeros_like(done)


def over_tp(array, k):
    return lax.ppermute(array, "tp", [(i, i ^ k) for i in range(4)])


def add_body(p2, p1, p3, p0, out):
    out[...] = p0[...] + p1[...] + p2[...] + p3[...]


def join_body(p0, p3, p1, p2, c_out, b_out):
    mine = lax.axis_index("tp")
    for k, piece in enumerate((p0, p1, p2, p3)):
        rows = pl.ds(pl.multiple_of(jnp.bitwise_xor(mine, k) * 128, 128), 128)
        c_out[rows, :] = piece[:, :WIDTH]
        b_out[rows, :] = piece[:, WIDTH:]


def on_device(inputs, b_proj, c_proj, logdecay, skip_gain, grad_out):
    tokens = inputs.shape[0]
    log_rows = logdecay.T
    gain = skip_gain.reshape(1, HEADS)
    x_heads, send_f, keep_f, middle_f, b_turned, levels, level_rows = summary(inputs, b_proj, log_rows)
    other_f = swap_cores(send_f)
    dy_heads, c_turned, middle_send, send_b = pulled_send(grad_out, c_proj, level_rows)
    other_b = swap_cores(send_b)
    half = (HALF, WIDTH, WIDTH)
    middle_b, keep_b = small(
        pulled_keep_body,
        [(HEADS, WIDTH, WIDTH), half],
        "summary_b_keep",
        dy_heads,
        c_turned,
        level_rows,
        middle_send,
        scratch=[half],
    )

    cores = (keep_f, other_f, keep_b, other_b)
    packed = (2, TALL, WIDTH)
    chips = small(core_up_body, [packed] * CHIPS, "core_up", *cores)
    local = (x_heads, dy_heads, b_proj, c_proj, levels, level_rows, gain)
    first = intra(0, *local, chips[0])
    chips = [along_chips(chips[k], k) for k in range(CHIPS)]
    (slab,) = small(slab_up_body, [packed], "slab_up", *taken(chips), scratch=[(CHIPS,) + packed], after=[first[-1]])
    other_slab = swap_cores(slab)
    unit = (WIDTH + LOG_ROWS, WIDTH)
    both, single = small(block_up_body, [(2,) + unit, unit], "block_up", slab, other_slab)
    single = to_far_block(single)
    both = to_near_blocks(both)
    entering = small(
        chip_down_body,
        [(2, 2 * WIDTH, WIDTH)] * CHIPS,
        "chip_down",
        *taken(chips),
        slab,
        other_slab,
        single,
        both,
        swap_cores(single),
        swap_cores(both),
        scratch=[(CHIPS,) + packed, (4, 2) + unit, (CHIPS, 2, 2 * WIDTH, WIDTH)],
    )
    y_part, dx_part, x_turned, dy_turned, near, base = intra(1, *local, entering[0], first)
    entering = [along_chips(entering[k], k) for k in range(CHIPS)]
    mine, theirs = small(
        core_down_body, [(HALF, 2 * WIDTH, WIDTH)] * 2, "core_down", *cores, *taken(entering), after=[base]
    )
    got = swap_cores(theirs)

    turned = (middle_f, middle_b, level_rows, x_turned, dy_turned, b_turned, c_turned)
    base, cross_own = grad_call(True, mine, *turned, base)
    pieces = grad_call(False, got, *turned, base)
    outputs, done = value_call(0, got, mine, middle_f, levels, c_proj, y_part, pieces[0])
    pieces = spread(pieces, over_tp)
    (start,) = small(start_body, [(HEADS, WIDTH)], "start", got, mine, send_b, keep_b, level_rows, after=[done])
    (cross_other,) = small(cross_body, [(HALF, tokens)], "cross_other", got, *turned, after=[start])
    (summed,) = small(add_body, [pieces[0].shape], "add", *taken(pieces), after=[cross_other])
    grad_inputs, done = value_call(1, got, mine, middle_b, levels, b_proj, dx_part, summed)
    decays, done = small(
        decay_body, [(HEADS, tokens), (8, WIDTH)], "decay", near, cross_own, cross_other, start, after=[done]
    )
    joined = spread([summed] * 4, over_tp)
    grad_c, grad_b = small(join_body, [(tokens, WIDTH)] * 2, "join", *reversed(taken(joined)), after=[done])
    return outputs, grad_inputs, decays.T, grad_b, grad_c


def solution(mesh):
    placed = (
        P("ctx", "tp", None),
        P("ctx", None),
        P("ctx", None),
        P("ctx", "tp"),
        P("tp"),
        P("ctx", "tp", None),
    )
    return jax.shard_map(
        on_device,
        mesh=mesh,
        in_specs=placed,
        out_specs=(
            P("ctx", "tp", None),
            P("ctx", "tp", None),
            P("ctx", "tp"),
            P("ctx", None),
            P("ctx", None),
        ),
        check_vma=False,
    )
```

```python
import functools

import jax
import jax.numpy as jnp
from jax import lax
from jax.experimental import pallas as pl
from jax.experimental.pallas import tpu as pltpu
from jax.sharding import PartitionSpec as P

SPAN = 256
HEADS = 16
HALF = 8
WIDTH = 128
CHIPS = 4
QUAD = 4
LOG_ROWS = 8
f32 = jnp.float32
bf16 = jnp.bfloat16
TALL = 2 * WIDTH + LOG_ROWS
anywhere = pl.BlockSpec(memory_space=pl.ANY)


def params():
    return pltpu.CompilerParams(vmem_limit_bytes=24 * 1024 * 1024)


def place():
    position = lax.axis_index("ctx")
    return position % 2, position // 2 % 4, position // 8


def dot(a, b, dims):
    return lax.dot_general(a, b, (dims, ((), ())), preferred_element_type=f32)


def split_two(a):
    high = a.astype(bf16)
    return high, (a - high.astype(f32)).astype(bf16)


def split_three(a):
    high = a.astype(bf16)
    rest = a - high.astype(f32)
    middle = rest.astype(bf16)
    return high, middle, (rest - middle.astype(f32)).astype(bf16)


def triangle(strict):
    row = lax.broadcasted_iota(jnp.int32, (SPAN, SPAN), 0)
    column = lax.broadcasted_iota(jnp.int32, (SPAN, SPAN), 1)
    kept = column < row if strict else column <= row
    return jnp.where(kept, 1.0, 0.0).astype(bf16)


def running_sum(rows, strict):
    count = rows.shape[0]
    sums = dot(jnp.concatenate(split_three(rows), axis=0), triangle(strict), ((1,), (1,)))
    return sums[:count] + sums[count : 2 * count] + sums[2 * count :]


def kept_half():
    core, _, depth = place()
    return jnp.bitwise_xor(core, depth % 2)


def fresh_state(proj_t, weight, value):
    weighted = jnp.concatenate(split_two(proj_t * weight), axis=0)
    both = dot(weighted, value, ((1,), (0,)))
    return both[:WIDTH] + both[WIDTH:]


def summary_body(values, proj_far, log_rows, *refs):
    heads_out, send, keep, middle, proj_out, levels_out, rows_all, here, proj, logs, total, arrived = refs
    copies = [
        pltpu.make_async_copy(log_rows, logs, arrived.at[0]),
        pltpu.make_async_copy(proj_far, proj, arrived.at[1]),
    ]
    copies += [
        pltpu.make_async_copy(values.at[pl.ds(span * SPAN, SPAN)], here.at[span], arrived.at[2 + span]) for span in (0, 1)
    ]
    for copy in copies:
        copy.start()
    copies[0].wait()
    sums = running_sum(jnp.concatenate([logs[:, :SPAN], logs[:, SPAN:]], axis=0), False)
    for span in (0, 1):
        tokens = slice(span * SPAN, span * SPAN + SPAN)
        level_rows = sums[span * HEADS : span * HEADS + HEADS]
        levels_out[tokens, :] = jnp.transpose(level_rows)
        rows_all[:, tokens] = level_rows
    copies[1].wait()
    last = [rows_all[:, SPAN * span + SPAN - 1 : SPAN * span + SPAN] for span in (0, 1)]
    carried = jnp.exp(last[1])
    all_log = last[0] + last[1]
    for span in (0, 1):
        tokens = slice(span * SPAN, span * SPAN + SPAN)
        weight = jnp.exp(last[span] - rows_all[:, tokens])
        proj_t = jnp.transpose(proj[tokens, :]).astype(f32)
        proj_out[:, tokens] = proj_t
        copies[2 + span].wait()
        swapped = jnp.swapaxes(here[span], 0, 1)
        heads_out[:, tokens, :] = swapped
        for head in range(HEADS):
            fresh = fresh_state(proj_t, weight[head : head + 1, :], swapped[head])
            if span == 0:
                middle[head] = fresh
            else:
                total[head] = fresh + carried[head : head + 1, :] * middle[head]
    kept = kept_half()
    for value in (0, 1):

        @pl.when(kept == value)
        def _():
            for out, half in ((keep, value), (send, 1 - value)):
                for at in range(HALF):
                    head = half * HALF + at
                    out[at, :WIDTH, :] = total[head]
                    out[at, WIDTH:, :] = jnp.broadcast_to(all_log[head : head + 1, :], (LOG_ROWS, WIDTH))


def summary(values, proj, log_rows):
    tokens = values.shape[0]
    packed = jax.ShapeDtypeStruct((HALF, WIDTH + LOG_ROWS, WIDTH), f32)
    return pl.pallas_call(
        summary_body,
        in_specs=[anywhere] * 3,
        out_shape=[
            jax.ShapeDtypeStruct((HEADS, tokens, WIDTH), bf16),
            packed,
            packed,
            jax.ShapeDtypeStruct((HEADS, WIDTH, WIDTH), f32),
            jax.ShapeDtypeStruct((WIDTH, tokens), f32),
            jax.ShapeDtypeStruct((tokens, HEADS), f32),
            jax.ShapeDtypeStruct((HEADS, tokens), f32),
        ],
        scratch_shapes=[
            pltpu.VMEM((2, SPAN, HEADS, WIDTH), bf16),
            pltpu.VMEM((tokens, WIDTH), bf16),
            pltpu.VMEM((HEADS, tokens), f32),
            pltpu.VMEM((HEADS, WIDTH, WIDTH), f32),
            pltpu.SemaphoreType.DMA((4,)),
        ],
        compiler_params=params(),
        name="summary_f",
    )(*[pltpu.with_memory_space_constraint(array, pltpu.HBM) for array in (values, proj, log_rows)])


def pulled_half(own, heads, proj_t, rows_all, middle, total):
    half = kept_half() if own else 1 - kept_half()
    rows = jnp.where(half == 0, rows_all[:HALF], rows_all[HALF:])
    carried = jnp.exp(rows[:, SPAN - 1 : SPAN])
    for span in (1, 0):
        tokens = slice(span * SPAN, span * SPAN + SPAN)
        weight = jnp.exp(rows[:, tokens])
        for at in range(HALF):
            fresh = fresh_state(proj_t[:, tokens], weight[at : at + 1, :], heads[half * HALF + at, tokens, :])
            if span == 1:
                middle[at] = fresh
            else:
                total[at] = fresh + carried[at : at + 1, :] * middle[at]


def pulled_send_body(values, proj, rows_all, heads_out, proj_out, middle, send):
    for span in (0, 1):
        tokens = slice(span * SPAN, span * SPAN + SPAN)
        proj_out[:, tokens] = jnp.transpose(proj[tokens, :]).astype(f32)
        heads_out[:, tokens, :] = jnp.swapaxes(values[tokens], 0, 1)
    pulled_half(False, heads_out, proj_out, rows_all, middle, send)


def pulled_keep_body(heads, proj_t, rows_all, middle_send, middle, keep, scratch):
    pulled_half(True, heads, proj_t, rows_all, scratch, keep)
    kept = kept_half()
    for at in range(HALF):
        middle[kept * HALF + at] = scratch[at]
        middle[(1 - kept) * HALF + at] = middle_send[at]


def pulled_send(values, proj, rows_all):
    tokens = values.shape[0]
    half = jax.ShapeDtypeStruct((HALF, WIDTH, WIDTH), f32)
    return pl.pallas_call(
        pulled_send_body,
        in_specs=[pl.BlockSpec(memory_space=pltpu.VMEM)] * 3,
        out_shape=[
            jax.ShapeDtypeStruct((HEADS, tokens, WIDTH), bf16),
            jax.ShapeDtypeStruct((WIDTH, tokens), f32),
            half,
            half,
        ],
        compiler_params=params(),
        name="summary_b_send",
    )(values, proj, rows_all)


def line_sums(product, head):
    row = lax.broadcasted_iota(jnp.int32, (2 * WIDTH, WIDTH), 1)
    picked = jnp.where(row == head, 1.0, 0.0).astype(bf16)
    return dot(jnp.concatenate(split_two(product), axis=1), picked, ((1,), (0,)))


def intra_body(x_ref, dy_ref, b_ref, c_ref, lev_ref, lev_rows_ref, gain_ref, *refs):
    y_out, dx_out, x_t_out, dy_t_out, cross_out, grads_out = refs[-6:]
    b = b_ref[...]
    c = c_ref[...]
    low, high = slice(0, 128), slice(128, 256)
    blocks = ((low, low), (high, low), (high, high))
    scores = [dot(c[t], b[s], ((1,), (1,))) for t, s in blocks]
    row = lax.broadcasted_iota(jnp.int32, (128, 128), 0)
    column = lax.broadcasted_iota(jnp.int32, (128, 128), 1)
    causal = column <= row
    score_grad = [jnp.zeros((128, 128), f32) for _ in blocks]
    cross = jnp.zeros((SPAN, WIDTH), f32)
    for head in range(HEADS):
        x = x_ref[head]
        dy = dy_ref[head]
        gain = gain_ref[:, head : head + 1]
        level = lev_ref[:, head : head + 1]
        level_row = lev_rows_ref[head : head + 1, :]
        mixing = []
        for at, (t, s) in enumerate(blocks):
            distance = level[t] - level_row[:, s]
            if t == s:
                distance = jnp.where(causal, distance, -1e30)
            decay = jnp.exp(distance)
            mixing.append((scores[at] * decay).astype(bf16))
            score_grad[at] = score_grad[at] + decay * dot(dy[t], x[s], ((1,), (1,)))
        lower = jnp.concatenate(mixing[1:], axis=1)
        left = jnp.concatenate(mixing[:2], axis=0)
        y = jnp.concatenate([dot(mixing[0], x[low], ((1,), (0,))), dot(lower, x, ((1,), (0,)))], axis=0)
        dx = jnp.concatenate([dot(left, dy, ((0,), (0,))), dot(mixing[2], dy[high], ((0,), (0,)))], axis=0)
        x32 = x.astype(f32)
        dy32 = dy.astype(f32)
        cross = cross + line_sums(y * dy32 - dx * x32, head)
        x_t_out[head] = jnp.transpose(x)
        dy_t_out[head] = jnp.transpose(dy)
        y_out[head] = y + gain * x32
        dx_out[head] = dx + gain * dy32
    cross_out[...] = jnp.transpose(cross[:, :HEADS])
    g00, g10, g11 = [split_two(g) for g in score_grad]
    grad_c0 = sum(dot(g, b[low], ((1,), (0,))) for g in g00)
    grad_c1 = sum(dot(g, b[low], ((1,), (0,))) for g in g10) + sum(dot(g, b[high], ((1,), (0,))) for g in g11)
    grad_b0 = sum(dot(g, c[low], ((0,), (0,))) for g in g00) + sum(dot(g, c[high], ((0,), (0,))) for g in g10)
    grad_b1 = sum(dot(g, c[high], ((0,), (0,))) for g in g11)
    grads_out[:WIDTH, low] = jnp.transpose(grad_c0)
    grads_out[:WIDTH, high] = jnp.transpose(grad_c1)
    grads_out[WIDTH:, low] = jnp.transpose(grad_b0)
    grads_out[WIDTH:, high] = jnp.transpose(grad_b1)


def intra(span, x_heads, dy_heads, b_proj, c_proj, levels, level_rows, gain, after, so_far=()):
    tokens = x_heads.shape[1]
    by_head = pl.BlockSpec((HEADS, SPAN, WIDTH), lambda s: (0, span, 0))
    flat = pl.BlockSpec((SPAN, WIDTH), lambda s: (span, 0))
    thin = pl.BlockSpec((SPAN, HEADS), lambda s: (span, 0))
    rows = pl.BlockSpec((HEADS, SPAN), lambda s: (0, span))
    turned = pl.BlockSpec((HEADS, WIDTH, SPAN), lambda s: (0, 0, span))
    turned_shape = jax.ShapeDtypeStruct((HEADS, WIDTH, tokens), bf16)
    return pl.pallas_call(
        intra_body,
        grid=(1,),
        in_specs=[
            by_head,
            by_head,
            flat,
            flat,
            thin,
            rows,
            pl.BlockSpec((1, HEADS), lambda s: (0, 0)),
            anywhere,
        ]
        + [anywhere] * len(so_far),
        out_specs=[by_head, by_head, turned, turned, rows, pl.BlockSpec((2 * WIDTH, SPAN), lambda s: (0, span))],
        out_shape=[
            jax.ShapeDtypeStruct((HEADS, tokens, WIDTH), f32),
            jax.ShapeDtypeStruct((HEADS, tokens, WIDTH), f32),
            turned_shape,
            turned_shape,
            jax.ShapeDtypeStruct((HEADS, tokens), f32),
            jax.ShapeDtypeStruct((2 * WIDTH, tokens), f32),
        ],
        input_output_aliases={8 + at: at for at in range(len(so_far))},
        compiler_params=params(),
        name="intra%d" % span,
    )(x_heads, dy_heads, b_proj, c_proj, levels, level_rows, gain, after, *so_far)


def small(body, outs, name, *args, scratch=(), after=()):
    count = len(args)

    def with_after(*refs):
        body(*refs[:count], *refs[count + len(after) :])

    return pl.pallas_call(
        with_after,
        in_specs=[pl.BlockSpec(memory_space=pltpu.VMEM)] * count + [anywhere] * len(after),
        out_shape=[jax.ShapeDtypeStruct(shape, f32) for shape in outs],
        scratch_shapes=[pltpu.VMEM(shape, f32) for shape in scratch],
        compiler_params=params(),
        name=name,
    )(*args, *after)


FORWARD = slice(0, WIDTH)
BACKWARD = slice(WIDTH, 2 * WIDTH)
LOGS = slice(2 * WIDTH, TALL)


def core_up_body(keep_f, other_f, keep_b, other_b, *outs):
    core, chip, _ = place()
    first = core == 0
    for k in range(CHIPS):
        for at in range(2):
            head = jnp.bitwise_xor(chip, k) * 2 + at
            own_log = keep_f[head, WIDTH:, :]
            other_log = other_f[head, WIDTH:, :]
            own_decay = jnp.exp(own_log)[:1]
            other_decay = jnp.exp(other_log)[:1]
            own_forward = jnp.where(first, other_decay, 1.0)
            other_forward = jnp.where(first, 1.0, own_decay)
            own_backward = jnp.where(first, 1.0, other_decay)
            other_backward = jnp.where(first, own_decay, 1.0)
            outs[k][at, FORWARD, :] = own_forward * keep_f[head, :WIDTH, :] + other_forward * other_f[head, :WIDTH, :]
            outs[k][at, BACKWARD, :] = own_backward * keep_b[head] + other_backward * other_b[head]
            outs[k][at, LOGS, :] = own_log + other_log


def chain(places, decays, states, entering):
    befores = {}
    for at in places:
        befores[at] = entering
        entering = decays[at] * entering + states(at)
    return befores, entering


TAKEN = (1, 3, 2, 0)


def taken(parts):
    return [parts[k] for k in TAKEN]


def untaken(parts):
    return [parts[TAKEN.index(k)] for k in range(4)]


def slab_up_body(*refs):
    parts, out, ordered = untaken(refs[:4]), refs[4], refs[5]
    _, chip, _ = place()
    zero = jnp.zeros((WIDTH, WIDTH), f32)
    for k in range(CHIPS):
        ordered[jnp.bitwise_xor(chip, k)] = parts[k][...]
    for head in range(2):
        logs = [ordered[at, head, LOGS, :] for at in range(CHIPS)]
        decays = [jnp.exp(log)[:1] for log in logs]
        out[head, FORWARD, :] = chain(range(4), decays, lambda at: ordered[at, head, FORWARD, :], zero)[1]
        out[head, BACKWARD, :] = chain(range(3, -1, -1), decays, lambda at: ordered[at, head, BACKWARD, :], zero)[1]
        out[head, LOGS, :] = sum(logs)


def in_slab_order(own, other):
    kept = kept_half()
    return jnp.where(kept == 0, own, other), jnp.where(kept == 0, other, own)


def block_up_body(own, other, both, single):
    core, _, depth = place()
    block = depth // 2
    near = jnp.bitwise_xor(block, jnp.where(core == 0, 1, 3))
    far = jnp.bitwise_xor(block, 2)
    for head in range(2):
        log0, log1 = in_slab_order(own[head, LOGS, :], other[head, LOGS, :])
        ahead0, ahead1 = in_slab_order(own[head, FORWARD, :], other[head, FORWARD, :])
        behind0, behind1 = in_slab_order(own[head, BACKWARD, :], other[head, BACKWARD, :])
        ahead = jnp.exp(log1)[:1] * ahead0 + ahead1
        behind = behind0 + jnp.exp(log0)[:1] * behind1
        both[head, :WIDTH, :] = jnp.where(near > block, ahead, behind)
        both[head, WIDTH:, :] = log0 + log1

        @pl.when(core == head)
        def _():
            single[:WIDTH, :] = jnp.where(far > block, ahead, behind)
            single[WIDTH:, :] = log0 + log1


def chip_down_body(*refs):
    parts, (own, other, single, both, other_single, other_both) = untaken(refs[:4]), refs[4:10]
    outs, ordered, came, entered = refs[10:14], *refs[14:]
    core, chip, depth = place()
    block = depth // 2
    kept = kept_half()
    for k in range(CHIPS):
        ordered[jnp.bitwise_xor(chip, k)] = parts[k][...]
    came[block] = jnp.zeros_like(came[0])
    came[jnp.bitwise_xor(block, jnp.where(core == 0, 1, 3))] = both[...]
    came[jnp.bitwise_xor(block, jnp.where(core == 0, 3, 1))] = other_both[...]
    far = jnp.bitwise_xor(block, 2)
    came[far, core] = single[...]
    came[far, 1 - core] = other_single[...]
    for head in range(2):
        decays = [jnp.exp(ordered[at, head, LOGS, :])[:1] for at in range(CHIPS)]
        for way, rows in ((0, FORWARD), (1, BACKWARD)):
            entering = jnp.zeros((WIDTH, WIDTH), f32)
            for at in range(3, -1, -1) if way else range(4):
                counts = at > block if way else at < block
                passed = jnp.exp(came[at, head, WIDTH:, :])[:1] * entering + came[at, head, :WIDTH, :]
                entering = jnp.where(counts, passed, entering)
            crossed = jnp.exp(other[head, LOGS, :])[:1] * entering + other[head, rows, :]
            entering = jnp.where(kept == 1 - way, crossed, entering)
            places = range(3, -1, -1) if way else range(4)
            befores, _ = chain(places, decays, lambda at: ordered[at, head, rows, :], entering)
            for at, before in befores.items():
                entered[at, head, rows, :] = before
    for k in range(CHIPS):
        outs[k][...] = entered[jnp.bitwise_xor(chip, k)]


def core_down_body(keep_f, other_f, keep_b, other_b, *refs):
    pieces, mine, theirs = untaken(refs[:4]), refs[4], refs[5]
    core, chip, _ = place()
    first = core == 0
    for k in range(CHIPS):
        for at in range(2):
            head = jnp.bitwise_xor(chip, k) * 2 + at
            forward = pieces[k][at, FORWARD, :]
            backward = pieces[k][at, BACKWARD, :]
            own_decay = jnp.exp(keep_f[head, WIDTH:, :])[:1]
            other_decay = jnp.exp(other_f[head, WIDTH:, :])[:1]
            mine[head, FORWARD, :] = jnp.where(first, forward, other_decay * forward + other_f[head, :WIDTH, :])
            mine[head, BACKWARD, :] = jnp.where(first, other_decay * backward + other_b[head], backward)
            theirs[head, FORWARD, :] = jnp.where(first, own_decay * forward + keep_f[head, :WIDTH, :], forward)
            theirs[head, BACKWARD, :] = jnp.where(first, backward, own_decay * backward + keep_b[head])


def over_ctx(array, target):
    return lax.ppermute(array, "ctx", [(i, target(i)) for i in range(64)])


def swap_cores(array):
    return over_ctx(array, lambda i: i ^ 1)


def along_chips(array, k):
    return over_ctx(array, lambda i: i ^ 2 * k ^ (8 if i % 2 else 0))


def to_near_blocks(array):
    return over_ctx(array, lambda i: i ^ (48 if i % 2 else 16))


def to_far_block(array):
    return over_ctx(array, lambda i: i ^ 32)


def spread(parts, move):
    return [parts[0]] + [move(parts[k], k) for k in range(1, len(parts))]


def half_of(own, array):
    half = kept_half() if own else 1 - kept_half()
    return jnp.where(half == 0, array[:HALF], array[HALF:])


def lines_of(own, span, way, states, middle, level_rows, values):
    half = kept_half() if own else 1 - kept_half()
    lanes = slice(span * SPAN, span * SPAN + SPAN)
    rows = half_of(own, level_rows[:, lanes])
    weight = jnp.exp(rows[:, SPAN - 1 : SPAN] - rows) if way else jnp.exp(rows)
    last = 2 * SPAN - 1 if way else SPAN - 1
    crossed = half_of(own, jnp.exp(level_rows[:, last : last + 1]))
    for at in range(HALF):
        head = half * HALF + at
        state = states[at, way * WIDTH : way * WIDTH + WIDTH, :]
        if span == 1 - way:
            state = crossed[at : at + 1, :] * state + middle[head]
        value = values[head, :, lanes]
        line = dot(
            jnp.concatenate(split_two(state), axis=1),
            jnp.concatenate([value, value], axis=0),
            ((1,), (0,)),
        )
        yield weight[at : at + 1, :], line


def grad_body(own, states, middle_f, middle_b, level_rows, x_turned, dy_turned, b_turned, c_turned, base, *refs):
    for span in range(2):
        lanes = slice(span * SPAN, span * SPAN + SPAN)
        crosses = []
        for way, middle, values, proj in ((0, middle_f, dy_turned, c_turned), (1, middle_b, x_turned, b_turned)):
            of_way = slice(way * WIDTH, way * WIDTH + WIDTH)
            acc = base[of_way, lanes]
            crosses.append([])
            for weight, line in lines_of(own, span, way, states, middle, level_rows, values):
                acc = acc + weight * line
                if own:
                    crosses[way].append(weight * jnp.sum(proj[:, lanes] * line, axis=0, keepdims=True))
            if own:
                refs[0][of_way, lanes] = acc
            else:
                refs[4][lanes, of_way] = jnp.transpose(acc)
        if own:
            for at in range(HALF):
                refs[1][at : at + 1, lanes] = crosses[0][at] - crosses[1][at]
    if not own:
        mine_tp = lax.axis_index("tp")
        for k in range(4):
            start = pl.multiple_of(jnp.bitwise_xor(mine_tp, k) * 128, 128)
            refs[k][...] = refs[4][pl.ds(start, 128), :]


def cross_body(states, middle_f, middle_b, level_rows, x_turned, dy_turned, b_turned, c_turned, out):
    for span in range(2):
        lanes = slice(span * SPAN, span * SPAN + SPAN)
        crosses = []
        for way, middle, values, proj in ((0, middle_f, dy_turned, c_turned), (1, middle_b, x_turned, b_turned)):
            lines = lines_of(False, span, way, states, middle, level_rows, values)
            crosses.append([weight * jnp.sum(proj[:, lanes] * line, axis=0, keepdims=True) for weight, line in lines])
        for at in range(HALF):
            out[at : at + 1, lanes] = crosses[0][at] - crosses[1][at]


def grad_call(own, states, *arrays):
    tokens = arrays[-1].shape[1]
    outs = [arrays[-1].shape, (HALF, tokens)] if own else [(tokens // 4, 2 * WIDTH)] * 4
    return small(
        functools.partial(grad_body, own),
        outs,
        "grads_own" if own else "grads_other",
        states,
        *arrays,
        scratch=[] if own else [(tokens, 2 * WIDTH)],
    )


def value_body(way, got, mine, middle, levels, proj, part, _, out, done, wide, turned, left):
    kept = kept_half()
    states = slice(way * WIDTH, way * WIDTH + WIDTH)
    last = 2 * SPAN - 1 if way else SPAN - 1
    crossed = jnp.exp(levels[last : last + 1, :])
    copies = []
    for span in range(2):
        tokens = slice(span * SPAN, span * SPAN + SPAN)
        level = levels[tokens, :]
        weight = jnp.exp(level[SPAN - 1 : SPAN, :] - level) if way else jnp.exp(level)
        doubled = jnp.concatenate([proj[tokens, :], proj[tokens, :]], axis=1)
        for head in range(HEADS):
            at = head % HALF
            state = jnp.where(head // HALF == kept, mine[at, states, :], got[at, states, :])
            if span == 1 - way:
                state = crossed[:, head : head + 1] * state + middle[head]
            far = dot(doubled, jnp.concatenate(split_two(state), axis=0), ((1,), (0,)))
            far = far * weight[:, head : head + 1]
            wide[span, head] = (part[head, tokens, :] + far).astype(bf16)
        turned[span] = jnp.swapaxes(wide[span], 0, 1)
        copies.append(pltpu.make_async_copy(turned.at[span], out.at[pl.ds(span * SPAN, SPAN)], left.at[span]))
        copies[-1].start()
    done[...] = jnp.zeros_like(done)
    for copy in copies:
        copy.wait()


def value_call(way, got, mine, middle, levels, proj, part, after):
    tokens = levels.shape[0]
    return pl.pallas_call(
        functools.partial(value_body, way),
        in_specs=[pl.BlockSpec(memory_space=pltpu.VMEM)] * 6 + [anywhere],
        out_specs=[anywhere, pl.BlockSpec(memory_space=pltpu.VMEM)],
        out_shape=[
            jax.ShapeDtypeStruct((tokens, HEADS, WIDTH), bf16),
            jax.ShapeDtypeStruct((8, WIDTH), f32),
        ],
        scratch_shapes=[
            pltpu.VMEM((2, HEADS, SPAN, WIDTH), bf16),
            pltpu.VMEM((2, SPAN, HEADS, WIDTH), bf16),
            pltpu.SemaphoreType.DMA((2,)),
        ],
        compiler_params=params(),
        name="values_b" if way else "values_f",
    )(got, mine, middle, levels, proj, part, after)


def start_body(got, mine, send_b, keep_b, level_rows, out):
    kept = kept_half()
    all_log = level_rows[:, SPAN - 1 : SPAN] + level_rows[:, 2 * SPAN - 1 : 2 * SPAN]
    for head in range(HEADS):
        at = head % HALF
        own = head // HALF == kept
        incoming = jnp.where(own, mine[at], got[at])
        local = jnp.where(own, keep_b[at], send_b[at])
        pulled = local + jnp.exp(all_log[head : head + 1, :]) * incoming[WIDTH:]
        line = jnp.sum(jnp.sum(incoming[:WIDTH] * pulled, axis=0, keepdims=True), axis=1, keepdims=True)
        out[head : head + 1, :] = jnp.broadcast_to(line, (1, WIDTH))


def decay_body(near, cross_own, cross_other, start_ref, out, done):
    kept = kept_half()
    start = start_ref[:, :1]
    for span in range(2):
        rows = slice(span * SPAN, span * SPAN + SPAN)
        own = cross_own[:, rows]
        other = cross_other[:, rows]
        far = jnp.concatenate([jnp.where(kept == 0, own, other), jnp.where(kept == 0, other, own)], axis=0)
        cross = near[:, rows] + far
        out[:, rows] = start - running_sum(cross, True)
        start = start - jnp.sum(cross, axis=1, keepdims=True)
    done[...] = jnp.zeros_like(done)


def over_tp(array, k):
    return lax.ppermute(array, "tp", [(i, i ^ k) for i in range(4)])


def add_body(p2, p1, p3, p0, out):
    out[...] = p0[...] + p1[...] + p2[...] + p3[...]


def join_body(p0, p2, p3, p1, c_out, b_out):
    mine = lax.axis_index("tp")
    for k, piece in enumerate((p0, p1, p2, p3)):
        rows = pl.ds(pl.multiple_of(jnp.bitwise_xor(mine, k) * 128, 128), 128)
        c_out[rows, :] = piece[:, :WIDTH]
        b_out[rows, :] = piece[:, WIDTH:]


def on_device(inputs, b_proj, c_proj, logdecay, skip_gain, grad_out):
    tokens = inputs.shape[0]
    log_rows = logdecay.T
    gain = skip_gain.reshape(1, HEADS)
    x_heads, send_f, keep_f, middle_f, b_turned, levels, level_rows = summary(inputs, b_proj, log_rows)
    other_f = swap_cores(send_f)
    dy_heads, c_turned, middle_send, send_b = pulled_send(grad_out, c_proj, level_rows)
    other_b = swap_cores(send_b)
    half = (HALF, WIDTH, WIDTH)
    middle_b, keep_b = small(
        pulled_keep_body,
        [(HEADS, WIDTH, WIDTH), half],
        "summary_b_keep",
        dy_heads,
        c_turned,
        level_rows,
        middle_send,
        scratch=[half],
    )

    cores = (keep_f, other_f, keep_b, other_b)
    packed = (2, TALL, WIDTH)
    chips = small(core_up_body, [packed] * CHIPS, "core_up", *cores)
    local = (x_heads, dy_heads, b_proj, c_proj, levels, level_rows, gain)
    first = intra(0, *local, chips[0])
    chips = [along_chips(chips[k], k) for k in range(CHIPS)]
    (slab,) = small(slab_up_body, [packed], "slab_up", *taken(chips), scratch=[(CHIPS,) + packed], after=[first[-1]])
    other_slab = swap_cores(slab)
    unit = (WIDTH + LOG_ROWS, WIDTH)
    both, single = small(block_up_body, [(2,) + unit, unit], "block_up", slab, other_slab)
    single = to_far_block(single)
    both = to_near_blocks(both)
    entering = small(
        chip_down_body,
        [(2, 2 * WIDTH, WIDTH)] * CHIPS,
        "chip_down",
        *taken(chips),
        slab,
        other_slab,
        single,
        both,
        swap_cores(single),
        swap_cores(both),
        scratch=[(CHIPS,) + packed, (4, 2) + unit, (CHIPS, 2, 2 * WIDTH, WIDTH)],
    )
    y_part, dx_part, x_turned, dy_turned, near, base = intra(1, *local, entering[0], first)
    entering = [along_chips(entering[k], k) for k in range(CHIPS)]
    mine, theirs = small(
        core_down_body, [(HALF, 2 * WIDTH, WIDTH)] * 2, "core_down", *cores, *taken(entering), after=[base]
    )
    got = swap_cores(theirs)

    turned = (middle_f, middle_b, level_rows, x_turned, dy_turned, b_turned, c_turned)
    base, cross_own = grad_call(True, mine, *turned, base)
    pieces = grad_call(False, got, *turned, base)
    outputs, done = value_call(0, got, mine, middle_f, levels, c_proj, y_part, pieces[0])
    pieces = spread(pieces, over_tp)
    (start,) = small(start_body, [(HEADS, WIDTH)], "start", got, mine, send_b, keep_b, level_rows, after=[done])
    (cross_other,) = small(cross_body, [(HALF, tokens)], "cross_other", got, *turned, after=[start])
    (summed,) = small(add_body, [pieces[0].shape], "add", *taken(pieces), after=[cross_other])
    grad_inputs, done = value_call(1, got, mine, middle_b, levels, b_proj, dx_part, summed)
    decays, done = small(
        decay_body, [(HEADS, tokens), (8, WIDTH)], "decay", near, cross_own, cross_other, start, after=[done]
    )
    joined = spread([summed] * 4, over_tp)
    grad_c, grad_b = small(join_body, [(tokens, WIDTH)] * 2, "join", *reversed(taken(joined)), after=[done])
    return outputs, grad_inputs, decays.T, grad_b, grad_c


def solution(mesh):
    placed = (
        P("ctx", "tp", None),
        P("ctx", None),
        P("ctx", None),
        P("ctx", "tp"),
        P("tp"),
        P("ctx", "tp", None),
    )
    return jax.shard_map(
        on_device,
        mesh=mesh,
        in_specs=placed,
        out_specs=(
            P("ctx", "tp", None),
            P("ctx", "tp", None),
            P("ctx", "tp"),
            P("ctx", None),
            P("ctx", None),
        ),
        check_vma=False,
    )
```
